32 devices in a mesh: clip: 16 (over z, x, core), tm: 2 (over y).
Axes of the slice: x: 2, y: 2, z: 4, core: 2. Of those that a mesh axis runs over, the one named last changes fastest.
Arguments:
- clip_in: bfloat16 [16, 4, 8, 32, 128], P('clip', 'tm'), may hold values from -6 to 6
- cotangent: bfloat16 [16, 4, 8, 32, 128], P('clip', 'tm'), may hold values from -6 to 6
- spatial_w: bfloat16 [3, 3, 128, 128], replicated, may hold values from -0.1875 to 0.1875
- spatial_b: float32 [128], replicated, may hold values from -3 to 3
- temporal_w: bfloat16 [3, 128, 128], replicated, may hold values from -0.3125 to 0.3125
Outputs:
- grad_input: bfloat16 [16, 4, 8, 32, 128], P('clip', 'tm')
- grad_spatial_w: float32 [3, 3, 128, 128], replicated
- grad_spatial_b: float32 [128], replicated
- grad_temporal_w: float32 [3, 128, 128], replicated
The draws below stay inside these ranges and needn't reach their ends.
All inputs are finite; a program needn't handle non-finite values.
Results may differ from the reference program's by a relative error of at most 0.006.
Values may be sent and summed in bfloat16 or wider, within the bound.
A program may use at most 64 MiB of HBM per device.

```python
import jax
import jax.numpy as jnp
from jax import lax

C = 128
W = 32
T_SIZE = 4
H = 8
CLIPS = 16


def steps_of(stream_key, dims, cuts, low, top_value):
    loudness, own = 1.0, jax.random.fold_in(stream_key, 6)
    for dim, blocks in cuts:
        heights = jnp.exp(jax.random.uniform(jax.random.fold_in(own, dim), (blocks,), jnp.float32, low / len(cuts), top_value / len(cuts)))
        loudness = loudness * jnp.repeat(heights, dims[dim] // blocks).reshape([-1 if axis == dim else 1 for axis in range(len(dims))])
    return loudness


def normal_values(key, extent, scale, most, cuts=(), kind=jnp.bfloat16):
    entries = scale * jax.random.normal(key, extent, jnp.float32)
    if cuts:
        entries = entries * steps_of(key, extent, cuts, -0.22, 0.18)
    return jnp.clip(entries, -most, most).astype(kind)


def setup_inputs(seed: int = 0) -> dict:
    key_list = jax.random.split(jax.random.key(seed), 6)
    clip_in = normal_values(key_list[0], (CLIPS, T_SIZE, H, W, C), 1.0, 6.0, ((0, 16), (1, 2)))
    cotangent = normal_values(key_list[1], (CLIPS, T_SIZE, H, W, C), 1.0, 6.0, ((0, 16), (1, 2)))
    spatial_w = normal_values(key_list[2], (3, 3, C, C), (9 * C) ** -0.5, 0.1875)
    spatial_b = normal_values(key_list[3], (C,), 0.7, 3.0, (), jnp.float32)
    temporal_w = normal_values(key_list[4], (3, C, C), (3 * C) ** -0.5, 0.3125)
    return {"clip_in": clip_in, "cotangent": cotangent, "spatial_w": spatial_w, "spatial_b": spatial_b, "temporal_w": temporal_w}


def spatial_forward(frames, weights, bias):
    count, height, width, chan = frames.shape
    padded = jnp.pad(frames, ((0, 0), (1, 1), (1, 1), (0, 0)))
    total = jnp.zeros((count * height * width, chan), jnp.float32)
    for i in range(3):
        for j in range(3):
            window = padded[:, i:i + height, j:j + width, :].reshape(-1, chan)
            total = total + jnp.dot(window, weights[i, j], preferred_element_type=jnp.float32)
    return (total + bias).reshape(count, height, width, chan)

def spatial_transpose(grads, weights):
    count, height, width, chan = grads.shape
    padded = jnp.pad(grads, ((0, 0), (1, 1), (1, 1), (0, 0)))
    total = jnp.zeros((count * height * width, chan), jnp.float32)
    for i in range(3):
        for j in range(3):
            window = padded[:, 2 - i:2 - i + height, 2 - j:2 - j + width, :].reshape(-1, chan)
            total = total + jnp.dot(window, weights[i, j].T, preferred_element_type=jnp.float32)
    return total.reshape(count, height, width, chan)

def spatial_weight_grad(frames, grads):
    count, height, width, chan = frames.shape
    padded = jnp.pad(frames, ((0, 0), (1, 1), (1, 1), (0, 0)))
    flat_grads = grads.reshape(-1, chan)
    result = []
    for i in range(3):
        row_terms = []
        for j in range(3):
            window = padded[:, i:i + height, j:j + width, :].reshape(-1, chan)
            row_terms.append(lax.dot_general(window, flat_grads, (((0,), (0,)), ((), ())), preferred_element_type=jnp.float32))
        result.append(jnp.stack(row_terms))
    return jnp.stack(result)

def one_clip(pieces, spatial_w, spatial_b, temporal_w):
    frames, cot = pieces
    count, height, width, chan = frames.shape
    pre = spatial_forward(frames, spatial_w, spatial_b)
    act = jax.nn.silu(pre).astype(jnp.bfloat16)
    later = jnp.concatenate([cot, jnp.zeros((2, height, width, chan), cot.dtype)], axis=0)
    earlier = jnp.concatenate([jnp.zeros((2, height, width, chan), act.dtype), act], axis=0)
    flat_cot = cot.reshape(-1, chan)
    grad_act = jnp.zeros((count * height * width, chan), jnp.float32)
    lag_terms = []
    for k in range(3):
        grad_act = grad_act + jnp.dot(later[k:k + count].reshape(-1, chan), temporal_w[k].T, preferred_element_type=jnp.float32)
        shifted = earlier[2 - k:2 - k + count].reshape(-1, chan)
        lag_terms.append(lax.dot_general(shifted, flat_cot, (((0,), (0,)), ((), ())), preferred_element_type=jnp.float32))
    grad_act = grad_act.astype(jnp.bfloat16).reshape(count, height, width, chan)
    sig = jax.nn.sigmoid(pre)
    grad_pre = (grad_act.astype(jnp.float32) * sig * (1.0 + pre * (1.0 - sig))).astype(jnp.bfloat16)
    grad_in = (cot.astype(jnp.float32) + spatial_transpose(grad_pre, spatial_w)).astype(jnp.bfloat16)
    grad_sw = spatial_weight_grad(frames, grad_pre)
    grad_sb = lax.optimization_barrier(jnp.sum(grad_pre.astype(jnp.float32).reshape(-1, chan), axis=0))
    return (grad_in, grad_sw, grad_sb, jnp.stack(lag_terms))

def reference(clip_in, cotangent, spatial_w, spatial_b, temporal_w):

    def work(pieces):
        return one_clip(pieces, spatial_w, spatial_b, temporal_w)
    grad_in, grad_sw, grad_sb, grad_tw = lax.map(work, (clip_in, cotangent))
    norm = 1.0 / jnp.sqrt(jnp.float32(CLIPS * T_SIZE * H * W))
    return (grad_in, lax.optimization_barrier(jnp.sum(grad_sw, axis=0)) * norm, lax.optimization_barrier(jnp.sum(grad_sb, axis=0)) * norm, lax.optimization_barrier(jnp.sum(grad_tw, axis=0)) * norm)
```

```python
import functools

import jax
import jax.numpy as jnp
from jax import lax
from jax.experimental import pallas as pl
from jax.experimental.pallas import tpu as pltpu
from jax.sharding import PartitionSpec as P

MESH = pl.DeviceIdType.MESH
F32, BF16 = jnp.float32, jnp.bfloat16
TILE = 16
CHUNKS = 1


def bits_of(size):
    count = size.bit_length() - 1
    assert 1 << count == size
    return count


def make_plan(clips, tms, rows):
    clip_bits, tm_bits = bits_of(clips), bits_of(tms)
    groups = [
        [("clip", 0)][:clip_bits],
        [("tm", b) for b in range(tm_bits)] + [("clip", b) for b in range(1, clip_bits) if b < 2],
        [("clip", b) for b in range(2, clip_bits)],
    ]
    plan = []
    for order, group in enumerate(groups):
        kind = F32 if order == 0 else BF16
        cut = len(group)
        while rows % (TILE << cut):
            cut -= 1
        if cut:
            plan.append((tuple(group[:cut]), True, rows, rows >> cut, kind))
            rows >>= cut
        if cut < len(group):
            plan.append((tuple(group[cut:]), False, rows, rows, kind))
    return plan


def kernel(plan, chunk_rows, tms, *refs):
    x_ref, cot_ref, sw_ref, sb_ref, tw_ref, gin_ref, grads_ref, bias_ref = refs[:8]
    next_cot, pad3, acc, res, cot_send, cot_recv = refs[8:14]
    phases, position = [], 14
    for _ in plan:
        phases.append(refs[position : position + 12])
        position += 12
    frames, height, width, chan = x_ref.shape[1:]
    area = height * width
    pixels = frames * area
    chunks = acc.shape[0]
    me = {"clip": lax.axis_index("clip"), "tm": lax.axis_index("tm")}

    def bit(which):
        axis, b = which
        return lax.rem(me[axis] // (1 << b), 2)

    def group_index(group):
        return sum((bit(w) * (1 << n) for n, w in enumerate(group)), 0)

    def partner(group, m):
        to = dict(me)
        index = group_index(group)
        for n, which in enumerate(group):
            if (m >> n) & 1:
                axis, b = which
                to[axis] = to[axis] + (1 - 2 * bit(which)) * (1 << b)
                index = index + (1 - 2 * bit(which)) * (1 << n)
        return to, index

    barrier = pltpu.get_barrier_semaphore()
    greeted = 0
    for group, *_ in plan:
        for m in range(1, 1 << len(group)):
            pl.semaphore_signal(barrier, inc=1, device_id=partner(group, m)[0], device_id_type=MESH)
            greeted += 1
    pl.semaphore_wait(barrier, greeted)

    tm = me["tm"]
    cot_copy = pltpu.make_async_remote_copy(
        src_ref=cot_ref.at[0, pl.ds(0, 2)],
        dst_ref=next_cot,
        send_sem=cot_send,
        recv_sem=cot_recv,
        device_id={"clip": me["clip"], "tm": jnp.maximum(tm - 1, 0)},
        device_id_type=MESH,
    )

    @pl.when(tm > 0)
    def _():
        cot_copy.start()

    column = lax.broadcasted_iota(jnp.int32, (pixels, chan), 0) % width

    def column_shift(flat, d):
        if d == 0:
            return flat.astype(BF16)
        rolled = pltpu.roll(flat, (-d) % pixels, 0)
        edge = width - 1 if d == 1 else 0
        return jnp.where(column == edge, 0.0, rolled).astype(BF16)

    def fill(flat, sign):
        for j in range(3):
            moved = column_shift(flat, sign * (j - 1)).reshape(frames, area, chan)
            pad3[:, pl.ds(width, area), pl.ds(j * chan, chan)] = moved

    def window(start):
        return pad3[:, pl.ds(start * width, area), :].reshape(pixels, 3 * chan)

    blank = jnp.zeros((frames, width, 3 * chan), BF16)
    pad3[:, pl.ds(0, width), :] = blank
    pad3[:, pl.ds(width + area, width), :] = blank

    x = x_ref[0].reshape(pixels, chan)
    fill(x.astype(F32), 1)
    pre = jnp.zeros((pixels, chan), F32)
    for i in range(3):
        pre = pre + jnp.dot(
            window(i), sw_ref[i].reshape(3 * chan, chan), preferred_element_type=F32
        )
    pre = pre + sb_ref[...]
    sig = 1.0 / (1.0 + jnp.exp(-pre))
    act = (pre * sig).astype(BF16)
    slope = sig * (1.0 + pre * (1.0 - sig))
    act_t = act.astype(F32).T.astype(BF16)
    x_t = x.astype(F32).T.astype(BF16)

    last = tm == tms - 1

    @pl.when(last)
    def _():
        next_cot[...] = jnp.zeros_like(next_cot)

    @pl.when(jnp.logical_not(last))
    def _():
        cot_copy.wait_recv()

    cot = cot_ref[0].reshape(pixels, chan)
    after = next_cot[...].reshape(2 * area, chan)
    later = [cot]
    for k in (1, 2):
        kept = [cot[k * area :]] if k < frames else []
        later.append(jnp.concatenate(kept + [after[: k * area]], axis=0))
    later = jnp.concatenate(later, axis=1)
    nt = (((1,), (1,)), ((), ()))
    tw = jnp.concatenate([tw_ref[k] for k in range(3)], axis=1)
    grad_act = lax.dot_general(later, tw, nt, preferred_element_type=F32).astype(BF16)
    grad_pre = (grad_act.astype(F32) * slope).astype(BF16)
    grad_pre32 = grad_pre.astype(F32)
    fill(grad_pre32, -1)

    def put(block, value):
        row = block * chan
        c = row // chunk_rows
        acc[c, pl.ds(row - c * chunk_rows, chan), :] = value

    grad_tw = jnp.dot(act_t, later, preferred_element_type=F32)
    for k in range(3):
        put(k, grad_tw[:, k * chan : (k + 1) * chan])

    def spatial_row(i):
        grad = jnp.dot(x_t, window(2 - i), preferred_element_type=F32)
        for j in range(3):
            put(3 + 3 * i + j, grad[:, j * chan : (j + 1) * chan])

    def input_grad():
        total = cot.astype(F32)
        for i in range(3):
            sw = jnp.concatenate([sw_ref[i, j] for j in range(3)], axis=1)
            total = total + lax.dot_general(window(2 - i), sw, nt, preferred_element_type=F32)
        gin_ref[0] = total.astype(BF16).reshape(frames, height, width, chan)

    offsets = [0]
    for group, scatter, _, share, _ in plan:
        offsets.append(offsets[-1] + (group_index(group) * share if scatter else 0))
    pending = []

    def start(copy):
        copy.start()
        pending.append(copy)
        return copy

    waiting = {}

    def share_at(index, share):
        return pl.ds(pl.multiple_of(index * share, TILE), share)

    def reduce_start(c, p):
        group, scatter, rows, share, kind = plan[p]
        cur, stage, recv, bsend, brecv = phases[p][:5]
        ss, rs, bss, brs = phases[p][6:10]
        index = group_index(group)
        source = cur
        if p == 0:
            source = acc
        if kind != F32:
            stage[c] = source[c].astype(kind)
            outgoing = stage
        else:
            outgoing = source
        copies = []
        for m in range(1, 1 << len(group)):
            to, their = partner(group, m)
            src = outgoing.at[c, share_at(their, share)] if scatter else outgoing.at[c]
            copies.append(
                start(
                    pltpu.make_async_remote_copy(
                        src_ref=src,
                        dst_ref=recv.at[c, index],
                        send_sem=ss.at[c, m],
                        recv_sem=rs.at[c, m],
                        device_id=to,
                        device_id_type=MESH,
                    )
                )
            )
            if c == chunks - 1:
                copies.append(
                    start(
                        pltpu.make_async_remote_copy(
                            src_ref=bsend,
                            dst_ref=brecv.at[index],
                            send_sem=bss.at[m],
                            recv_sem=brs.at[m],
                            device_id=to,
                            device_id_type=MESH,
                        )
                    )
                )
        waiting[c] = copies

    def reduce_end(c, p):
        group, scatter, rows, share, kind = plan[p]
        cur, stage, recv, bsend, brecv = phases[p][:5]
        index = group_index(group)
        source = acc if p == 0 else cur
        own = source[c, share_at(index, share)] if scatter else source[c]
        recv[c, index] = own.astype(kind)
        if c == chunks - 1:
            brecv[index] = bsend[...]
        for copy in waiting[c]:
            copy.wait_recv()
        total = recv[c, 0].astype(F32)
        for n in range(1, 1 << len(group)):
            total = total + recv[c, n].astype(F32)
        if c == chunks - 1:
            bias = brecv[0]
            for n in range(1, 1 << len(group)):
                bias = bias + brecv[n]
            if p + 1 < len(plan):
                phases[p + 1][3][...] = bias
            else:
                bias_ref[...] = bias
        if p + 1 < len(plan):
            phases[p + 1][0][c] = total
        else:
            res[c, pl.ds(pl.multiple_of(offsets[-1], TILE), share)] = total.astype(BF16)

    def gather_start(c, p):
        group, scatter, rows, share, kind = plan[p]
        gs, gr = phases[p][10:12]
        copies = []
        mine = res.at[c, pl.ds(pl.multiple_of(offsets[p + 1], TILE), share)]
        for m in range(1, 1 << len(group)):
            to, _ = partner(group, m)
            copies.append(
                start(
                    pltpu.make_async_remote_copy(
                        src_ref=mine,
                        dst_ref=mine,
                        send_sem=gs.at[c, m],
                        recv_sem=gr.at[c, m],
                        device_id=to,
                        device_id_type=MESH,
                    )
                )
            )
        waiting[c] = copies

    def gather_end(c, p):
        for copy in waiting[c]:
            copy.wait_recv()

    steps = []
    for p in range(len(plan)):
        steps.append((reduce_start, reduce_end, p))
    for p in reversed(range(len(plan))):
        if plan[p][1]:
            steps.append((gather_start, gather_end, p))

    def advance(c, k):
        if k > 0:
            steps[k - 1][1](c, steps[k - 1][2])
        if k < len(steps):
            steps[k][0](c, steps[k][2])
        else:
            grads_ref[pl.ds(c * chunk_rows, chunk_rows)] = res[c]

    phases[0][3][...] = jnp.sum(grad_pre32.reshape(pixels // 8, 8, chan), axis=0)
    for i in range(3):
        spatial_row(i)
    for c in range(chunks):
        advance(c, 0)
    input_grad()
    for step in range(1, len(steps) + chunks):
        for c in range(chunks):
            if 1 <= step - c <= len(steps):
                advance(c, step - c)
    for copy in pending:
        copy.wait_send()

    @pl.when(tm > 0)
    def _():
        cot_copy.wait_send()


def local(clips, tms, clip_in, cotangent, spatial_w, spatial_b, temporal_w):
    _, frames, height, width, chan = clip_in.shape
    assert frames == 2
    total_rows = 12 * chan
    chunk_rows = total_rows // CHUNKS
    plan = make_plan(clips, tms, chunk_rows)
    scratch = [
        pltpu.VMEM((2, height, width, chan), BF16),
        pltpu.VMEM((frames, (height + 2) * width, 3 * chan), BF16),
        pltpu.VMEM((CHUNKS, chunk_rows, chan), F32),
        pltpu.VMEM((CHUNKS, chunk_rows, chan), BF16),
        pltpu.SemaphoreType.DMA,
        pltpu.SemaphoreType.DMA,
    ]
    for order, (group, scatter, rows, share, kind) in enumerate(plan):
        n = 1 << len(group)
        sems = pltpu.SemaphoreType.DMA((CHUNKS, n))
        scratch += [
            pltpu.VMEM((CHUNKS, rows, chan) if order else (1, 8, chan), F32),
            pltpu.VMEM((CHUNKS, rows, chan) if kind != F32 else (1, TILE, chan), BF16),
            pltpu.VMEM((CHUNKS, n, share, chan), kind),
            pltpu.VMEM((8, chan), F32),
            pltpu.VMEM((n, 8, chan), F32),
            pltpu.VMEM((8, chan), F32),
            sems,
            sems,
            pltpu.SemaphoreType.DMA((n,)),
            pltpu.SemaphoreType.DMA((n,)),
            sems,
            sems,
        ]
    vmem = pl.BlockSpec(memory_space=pltpu.VMEM)
    grad_in, grads, bias = pl.pallas_call(
        functools.partial(kernel, plan, chunk_rows, tms),
        out_shape=(
            jax.ShapeDtypeStruct(clip_in.shape, BF16),
            jax.ShapeDtypeStruct((total_rows, chan), BF16),
            jax.ShapeDtypeStruct((8, chan), F32),
        ),
        in_specs=[vmem] * 5,
        out_specs=(vmem, vmem, vmem),
        scratch_shapes=scratch,
        compiler_params=pltpu.CompilerParams(
            collective_id=0, has_side_effects=True, vmem_limit_bytes=48 * 1024 * 1024
        ),
        name="block_backward",
    )(clip_in, cotangent, spatial_w, spatial_b.reshape(1, chan), temporal_w)
    norm = 1.0 / jnp.sqrt(F32(clips * tms * frames * height * width))
    grads = grads.astype(F32) * norm
    return (
        grad_in,
        grads[3 * chan :].reshape(3, 3, chan, chan),
        jnp.sum(bias, axis=0) * norm,
        grads[: 3 * chan].reshape(3, chan, chan),
    )


def solution(mesh):
    block = P("clip", "tm", None, None, None)
    return jax.shard_map(
        functools.partial(local, mesh.shape["clip"], mesh.shape["tm"]),
        mesh=mesh,
        in_specs=(block, block, P(), P(), P()),
        out_specs=(block, P(), P(), P()),
        check_vma=False,
    )
```

```python
import functools

import jax
import jax.numpy as jnp
from jax import lax
from jax.experimental import pallas as pl
from jax.experimental.pallas import tpu as pltpu
from jax.sharding import PartitionSpec as P

MESH = pl.DeviceIdType.MESH
F32, BF16 = jnp.float32, jnp.bfloat16
TILE = 16
CHUNKS = 1


def bits_of(size):
    count = size.bit_length() - 1
    assert 1 << count == size
    return count


def make_plan(clips, tms, rows):
    clip_bits, tm_bits = bits_of(clips), bits_of(tms)
    groups = [
        [("clip", 0)][:clip_bits],
        [("tm", b) for b in range(tm_bits)] + [("clip", b) for b in range(1, clip_bits) if b < 2],
        [("clip", b) for b in range(2, clip_bits)],
    ]
    plan = []
    for order, group in enumerate(groups):
        kind = F32 if order == 0 else BF16
        cut = len(group)
        while rows % (TILE << cut):
            cut -= 1
        if cut:
            plan.append((tuple(group[:cut]), True, rows, rows >> cut, kind))
            rows >>= cut
        if cut < len(group):
            plan.append((tuple(group[cut:]), False, rows, rows, kind))
    return plan


def kernel(plan, chunk_rows, tms, *refs):
    operands = refs[:5]
    gin_ref, grads_ref, bias_ref = refs[5:8]
    x_ref, cot_ref, sw_ref, sb_ref, tw_ref = held = refs[8:13]
    held_sems = refs[13]
    next_cot, pad3, acc, res, cot_send, cot_recv = refs[14:20]
    phases, position = [], 20
    for _ in plan:
        phases.append(refs[position : position + 12])
        position += 12
    frames, height, width, chan = x_ref.shape[1:]
    area = height * width
    pixels = frames * area
    chunks = acc.shape[0]
    me = {"clip": lax.axis_index("clip"), "tm": lax.axis_index("tm")}

    def bit(which):
        axis, b = which
        return lax.rem(me[axis] // (1 << b), 2)

    def group_index(group):
        return sum((bit(w) * (1 << n) for n, w in enumerate(group)), 0)

    def partner(group, m):
        to = dict(me)
        index = group_index(group)
        for n, which in enumerate(group):
            if (m >> n) & 1:
                axis, b = which
                to[axis] = to[axis] + (1 - 2 * bit(which)) * (1 << b)
                index = index + (1 - 2 * bit(which)) * (1 << n)
        return to, index

    barrier = pltpu.get_barrier_semaphore()
    greeted = 0
    for group, *_ in plan:
        for m in range(1, 1 << len(group)):
            pl.semaphore_signal(barrier, inc=1, device_id=partner(group, m)[0], device_id_type=MESH)
            greeted += 1
    x_in, cot_in, sw_in, sb_in, tw_in = fetch = [
        pltpu.make_async_copy(operand, copy, held_sems.at[n])
        for n, (operand, copy) in enumerate(zip(operands, held))
    ]
    for n in (0, 2, 3, 1, 4):
        fetch[n].start()
    pl.semaphore_wait(barrier, greeted)

    tm = me["tm"]
    cot_copy = pltpu.make_async_remote_copy(
        src_ref=operands[1].at[0, pl.ds(0, 2)],
        dst_ref=next_cot,
        send_sem=cot_send,
        recv_sem=cot_recv,
        device_id={"clip": me["clip"], "tm": jnp.maximum(tm - 1, 0)},
        device_id_type=MESH,
    )

    @pl.when(tm > 0)
    def _():
        cot_copy.start()

    column = lax.broadcasted_iota(jnp.int32, (pixels, chan), 0) % width

    def column_shift(flat, d):
        if d == 0:
            return flat.astype(BF16)
        rolled = pltpu.roll(flat, (-d) % pixels, 0)
        edge = width - 1 if d == 1 else 0
        return jnp.where(column == edge, 0.0, rolled).astype(BF16)

    def fill(flat, sign):
        for j in range(3):
            moved = column_shift(flat, sign * (j - 1)).reshape(frames, area, chan)
            pad3[:, pl.ds(width, area), pl.ds(j * chan, chan)] = moved

    def window(start):
        return pad3[:, pl.ds(start * width, area), :].reshape(pixels, 3 * chan)

    blank = jnp.zeros((frames, width, 3 * chan), BF16)
    pad3[:, pl.ds(0, width), :] = blank
    pad3[:, pl.ds(width + area, width), :] = blank

    x_in.wait()
    x = x_ref[0].reshape(pixels, chan)
    fill(x.astype(F32), 1)
    sw_in.wait()
    sb_in.wait()
    pre = jnp.zeros((pixels, chan), F32)
    for i in range(3):
        pre = pre + jnp.dot(
            window(i), sw_ref[i].reshape(3 * chan, chan), preferred_element_type=F32
        )
    pre = pre + sb_ref[...]
    sig = 1.0 / (1.0 + jnp.exp(-pre))
    act = (pre * sig).astype(BF16)
    slope = sig * (1.0 + pre * (1.0 - sig))
    act_t = act.astype(F32).T.astype(BF16)
    x_t = x.astype(F32).T.astype(BF16)

    cot_in.wait()
    tw_in.wait()
    last = tm == tms - 1

    @pl.when(last)
    def _():
        next_cot[...] = jnp.zeros_like(next_cot)

    @pl.when(jnp.logical_not(last))
    def _():
        cot_copy.wait_recv()

    cot = cot_ref[0].reshape(pixels, chan)
    after = next_cot[...].reshape(2 * area, chan)
    later = [cot]
    for k in (1, 2):
        kept = [cot[k * area :]] if k < frames else []
        later.append(jnp.concatenate(kept + [after[: k * area]], axis=0))
    later = jnp.concatenate(later, axis=1)
    nt = (((1,), (1,)), ((), ()))
    tw = jnp.concatenate([tw_ref[k] for k in range(3)], axis=1)
    grad_act = lax.dot_general(later, tw, nt, preferred_element_type=F32).astype(BF16)
    grad_pre = (grad_act.astype(F32) * slope).astype(BF16)
    grad_pre32 = grad_pre.astype(F32)
    fill(grad_pre32, -1)

    def put(block, value):
        row = block * chan
        c = row // chunk_rows
        acc[c, pl.ds(row - c * chunk_rows, chan), :] = value

    grad_tw = jnp.dot(act_t, later, preferred_element_type=F32)
    for k in range(3):
        put(k, grad_tw[:, k * chan : (k + 1) * chan])

    def spatial_row(i):
        grad = jnp.dot(x_t, window(2 - i), preferred_element_type=F32)
        for j in range(3):
            put(3 + 3 * i + j, grad[:, j * chan : (j + 1) * chan])

    def input_grad():
        total = cot.astype(F32)
        for i in range(3):
            sw = jnp.concatenate([sw_ref[i, j] for j in range(3)], axis=1)
            total = total + lax.dot_general(window(2 - i), sw, nt, preferred_element_type=F32)
        gin_ref[0] = total.astype(BF16).reshape(frames, height, width, chan)

    offsets = [0]
    for group, scatter, _, share, _ in plan:
        offsets.append(offsets[-1] + (group_index(group) * share if scatter else 0))
    pending = []

    def start(copy):
        copy.start()
        pending.append(copy)
        return copy

    waiting = {}

    def share_at(index, share):
        return pl.ds(pl.multiple_of(index * share, TILE), share)

    def reduce_start(c, p):
        group, scatter, rows, share, kind = plan[p]
        cur, stage, recv, bsend, brecv = phases[p][:5]
        ss, rs, bss, brs = phases[p][6:10]
        index = group_index(group)
        source = cur
        if p == 0:
            source = acc
        if kind != F32:
            stage[c] = source[c].astype(kind)
            outgoing = stage
        else:
            outgoing = source
        copies = []
        for m in range(1, 1 << len(group)):
            to, their = partner(group, m)
            src = outgoing.at[c, share_at(their, share)] if scatter else outgoing.at[c]
            copies.append(
                start(
                    pltpu.make_async_remote_copy(
                        src_ref=src,
                        dst_ref=recv.at[c, index],
                        send_sem=ss.at[c, m],
                        recv_sem=rs.at[c, m],
                        device_id=to,
                        device_id_type=MESH,
                    )
                )
            )
            if c == chunks - 1:
                copies.append(
                    start(
                        pltpu.make_async_remote_copy(
                            src_ref=bsend,
                            dst_ref=brecv.at[index],
                            send_sem=bss.at[m],
                            recv_sem=brs.at[m],
                            device_id=to,
                            device_id_type=MESH,
                        )
                    )
                )
        waiting[c] = copies

    def reduce_end(c, p):
        group, scatter, rows, share, kind = plan[p]
        cur, stage, recv, bsend, brecv = phases[p][:5]
        index = group_index(group)
        source = acc if p == 0 else cur
        own = source[c, share_at(index, share)] if scatter else source[c]
        recv[c, index] = own.astype(kind)
        if c == chunks - 1:
            brecv[index] = bsend[...]
        for copy in waiting[c]:
            copy.wait_recv()
        total = recv[c, 0].astype(F32)
        for n in range(1, 1 << len(group)):
            total = total + recv[c, n].astype(F32)
        if c == chunks - 1:
            bias = brecv[0]
            for n in range(1, 1 << len(group)):
                bias = bias + brecv[n]
            if p + 1 < len(plan):
                phases[p + 1][3][...] = bias
            else:
                bias_ref[...] = bias
        if p + 1 < len(plan):
            phases[p + 1][0][c] = total
        else:
            res[c, pl.ds(pl.multiple_of(offsets[-1], TILE), share)] = total.astype(BF16)

    def gather_start(c, p):
        group, scatter, rows, share, kind = plan[p]
        gs, gr = phases[p][10:12]
        copies = []
        mine = res.at[c, pl.ds(pl.multiple_of(offsets[p + 1], TILE), share)]
        for m in range(1, 1 << len(group)):
            to, _ = partner(group, m)
            copies.append(
                start(
                    pltpu.make_async_remote_copy(
                        src_ref=mine,
                        dst_ref=mine,
                        send_sem=gs.at[c, m],
                        recv_sem=gr.at[c, m],
                        device_id=to,
                        device_id_type=MESH,
                    )
                )
            )
        waiting[c] = copies

    def gather_end(c, p):
        for copy in waiting[c]:
            copy.wait_recv()

    steps = []
    for p in range(len(plan)):
        steps.append((reduce_start, reduce_end, p))
    for p in reversed(range(len(plan))):
        if plan[p][1]:
            steps.append((gather_start, gather_end, p))

    def advance(c, k):
        if k > 0:
            steps[k - 1][1](c, steps[k - 1][2])
        if k < len(steps):
            steps[k][0](c, steps[k][2])
        else:
            grads_ref[pl.ds(c * chunk_rows, chunk_rows)] = res[c]

    phases[0][3][...] = jnp.sum(grad_pre32.reshape(pixels // 8, 8, chan), axis=0)
    for i in range(3):
        spatial_row(i)
    for c in range(chunks):
        advance(c, 0)
    input_grad()
    for step in range(1, len(steps) + chunks):
        for c in range(chunks):
            if 1 <= step - c <= len(steps):
                advance(c, step - c)
    for copy in pending:
        copy.wait_send()

    @pl.when(tm > 0)
    def _():
        cot_copy.wait_send()


def finish(cells, gin_ref, grads_ref, bias_ref, gin_out, sw_out, sb_out, tw_out, sw, sb, tw, sems):
    norm = 1.0 / float(cells) ** 0.5
    chan = gin_ref.shape[-1]
    copies = [pltpu.make_async_copy(gin_ref, gin_out, sems.at[0])]
    copies[0].start()
    for k in range(3):
        tw[k] = grads_ref[k * chan : (k + 1) * chan].astype(F32) * norm
    copies.append(pltpu.make_async_copy(tw, tw_out, sems.at[1]))
    copies[1].start()
    sb[...] = jnp.sum(bias_ref[...], axis=0, keepdims=True) * norm
    copies.append(pltpu.make_async_copy(sb, sb_out, sems.at[2]))
    copies[2].start()
    for i in range(3):
        for j in range(3):
            row = (3 + 3 * i + j) * chan
            sw[i, j] = grads_ref[row : row + chan].astype(F32) * norm
    copies.append(pltpu.make_async_copy(sw, sw_out, sems.at[3]))
    copies[3].start()
    for copy in copies:
        copy.wait()


def local(clips, tms, clip_in, cotangent, spatial_w, spatial_b, temporal_w):
    _, frames, height, width, chan = clip_in.shape
    assert frames == 2
    total_rows = 12 * chan
    chunk_rows = total_rows // CHUNKS
    plan = make_plan(clips, tms, chunk_rows)
    operands = (clip_in, cotangent, spatial_w, spatial_b.reshape(1, chan), temporal_w)
    scratch = [pltpu.VMEM(a.shape, a.dtype) for a in operands] + [
        pltpu.SemaphoreType.DMA((5,)),
        pltpu.VMEM((2, height, width, chan), BF16),
        pltpu.VMEM((frames, (height + 2) * width, 3 * chan), BF16),
        pltpu.VMEM((CHUNKS, chunk_rows, chan), F32),
        pltpu.VMEM((CHUNKS, chunk_rows, chan), BF16),
        pltpu.SemaphoreType.DMA,
        pltpu.SemaphoreType.DMA,
    ]
    for order, (group, scatter, rows, share, kind) in enumerate(plan):
        n = 1 << len(group)
        sems = pltpu.SemaphoreType.DMA((CHUNKS, n))
        scratch += [
            pltpu.VMEM((CHUNKS, rows, chan) if order else (1, 8, chan), F32),
            pltpu.VMEM((CHUNKS, rows, chan) if kind != F32 else (1, TILE, chan), BF16),
            pltpu.VMEM((CHUNKS, n, share, chan), kind),
            pltpu.VMEM((8, chan), F32),
            pltpu.VMEM((n, 8, chan), F32),
            pltpu.VMEM((8, chan), F32),
            sems,
            sems,
            pltpu.SemaphoreType.DMA((n,)),
            pltpu.SemaphoreType.DMA((n,)),
            sems,
            sems,
        ]
    vmem = pl.BlockSpec(memory_space=pltpu.VMEM)
    grad_in, grads, bias = pl.pallas_call(
        functools.partial(kernel, plan, chunk_rows, tms),
        out_shape=(
            jax.ShapeDtypeStruct(clip_in.shape, BF16),
            jax.ShapeDtypeStruct((total_rows, chan), BF16),
            jax.ShapeDtypeStruct((8, chan), F32),
        ),
        in_specs=[pl.BlockSpec(memory_space=pltpu.HBM)] * 5,
        out_specs=(vmem, vmem, vmem),
        scratch_shapes=scratch,
        compiler_params=pltpu.CompilerParams(
            collective_id=0, has_side_effects=True, vmem_limit_bytes=48 * 1024 * 1024
        ),
        name="block_backward",
    )(*[pltpu.with_memory_space_constraint(a, pltpu.HBM) for a in operands])
    hbm = pl.BlockSpec(memory_space=pltpu.HBM)
    shapes = [(clip_in.shape, BF16), (spatial_w.shape, F32), ((1, chan), F32), (temporal_w.shape, F32)]
    cells = clips * tms * frames * height * width
    grad_in, grad_sw, grad_sb, grad_tw = pl.pallas_call(
        functools.partial(finish, cells),
        out_shape=[jax.ShapeDtypeStruct(*s) for s in shapes],
        in_specs=[vmem] * 3,
        out_specs=[hbm] * 4,
        scratch_shapes=[pltpu.VMEM(*s) for s in shapes[1:]] + [pltpu.SemaphoreType.DMA((4,))],
        compiler_params=pltpu.CompilerParams(vmem_limit_bytes=24 * 1024 * 1024),
        name="finish",
    )(grad_in, grads, bias)
    return grad_in, grad_sw, grad_sb.reshape(chan), grad_tw


def solution(mesh):
    block = P("clip", "tm", None, None, None)
    return jax.shard_map(
        functools.partial(local, mesh.shape["clip"], mesh.shape["tm"]),
        mesh=mesh,
        in_specs=(block, block, P(), P(), P()),
        out_specs=(block, P(), P(), P()),
        check_vma=False,
    )
```

```python
import functools

import jax
import jax.numpy as jnp
from jax import lax
from jax.experimental import pallas as pl
from jax.experimental.pallas import tpu as pltpu
from jax.sharding import PartitionSpec as P

MESH = pl.DeviceIdType.MESH
F32, BF16 = jnp.float32, jnp.bfloat16
TILE = 16
CHUNKS = 3


def bits_of(size):
    count = size.bit_length() - 1
    assert 1 << count == size
    return count


def make_plan(clips, tms, rows):
    clip_bits, tm_bits = bits_of(clips), bits_of(tms)
    groups = [
        [("clip", 0)][:clip_bits],
        [("tm", b) for b in range(tm_bits)] + [("clip", b) for b in range(1, clip_bits) if b < 2],
        [("clip", b) for b in range(2, clip_bits)],
    ]
    plan = []
    for order, group in enumerate(groups):
        kind = F32 if order == 0 else BF16
        cut = len(group)
        while rows % (TILE << cut):
            cut -= 1
        if cut:
            plan.append((tuple(group[:cut]), True, rows, rows >> cut, kind))
            rows >>= cut
        if cut < len(group):
            plan.append((tuple(group[cut:]), False, rows, rows, kind))
    return plan


def kernel(plan, chunk_rows, tms, *refs):
    operands = refs[:5]
    gin_ref, grads_ref, bias_ref = refs[5:8]
    x_ref, cot_ref, sw_ref, sb_ref, tw_ref = held = refs[8:13]
    held_sems = refs[13]
    next_cot, pad3, acc, res, cot_send, cot_recv = refs[14:20]
    phases, position = [], 20
    for _ in plan:
        phases.append(refs[position : position + 12])
        position += 12
    frames, height, width, chan = x_ref.shape[1:]
    area = height * width
    pixels = frames * area
    chunks = acc.shape[0]
    me = {"clip": lax.axis_index("clip"), "tm": lax.axis_index("tm")}

    def bit(which):
        axis, b = which
        return lax.rem(me[axis] // (1 << b), 2)

    def group_index(group):
        return sum((bit(w) * (1 << n) for n, w in enumerate(group)), 0)

    def partner(group, m):
        to = dict(me)
        index = group_index(group)
        for n, which in enumerate(group):
            if (m >> n) & 1:
                axis, b = which
                to[axis] = to[axis] + (1 - 2 * bit(which)) * (1 << b)
                index = index + (1 - 2 * bit(which)) * (1 << n)
        return to, index

    barrier = pltpu.get_barrier_semaphore()
    greeted = 0
    for group, *_ in plan:
        for m in range(1, 1 << len(group)):
            pl.semaphore_signal(barrier, inc=1, device_id=partner(group, m)[0], device_id_type=MESH)
            greeted += 1
    x_in, cot_in, sw_in, sb_in, tw_in = fetch = [
        pltpu.make_async_copy(operand, copy, held_sems.at[n])
        for n, (operand, copy) in enumerate(zip(operands, held))
    ]
    for n in (0, 2, 3, 1, 4):
        fetch[n].start()
    pl.semaphore_wait(barrier, greeted)

    tm = me["tm"]
    cot_copy = pltpu.make_async_remote_copy(
        src_ref=operands[1].at[0, pl.ds(0, 2)],
        dst_ref=next_cot,
        send_sem=cot_send,
        recv_sem=cot_recv,
        device_id={"clip": me["clip"], "tm": jnp.maximum(tm - 1, 0)},
        device_id_type=MESH,
    )

    @pl.when(tm > 0)
    def _():
        cot_copy.start()

    column = lax.broadcasted_iota(jnp.int32, (pixels, chan), 0) % width

    def column_shift(flat, d):
        if d == 0:
            return flat.astype(BF16)
        rolled = pltpu.roll(flat, (-d) % pixels, 0)
        edge = width - 1 if d == 1 else 0
        return jnp.where(column == edge, 0.0, rolled).astype(BF16)

    def fill(flat, sign):
        for j in range(3):
            moved = column_shift(flat, sign * (j - 1)).reshape(frames, area, chan)
            pad3[:, pl.ds(width, area), pl.ds(j * chan, chan)] = moved

    def window(start):
        return pad3[:, pl.ds(start * width, area), :].reshape(pixels, 3 * chan)

    blank = jnp.zeros((frames, width, 3 * chan), BF16)
    pad3[:, pl.ds(0, width), :] = blank
    pad3[:, pl.ds(width + area, width), :] = blank

    x_in.wait()
    x = x_ref[0].reshape(pixels, chan)
    fill(x.astype(F32), 1)
    sw_in.wait()
    sb_in.wait()
    pre = jnp.zeros((pixels, chan), F32)
    for i in range(3):
        pre = pre + jnp.dot(
            window(i), sw_ref[i].reshape(3 * chan, chan), preferred_element_type=F32
        )
    pre = pre + sb_ref[...]
    sig = 1.0 / (1.0 + jnp.exp(-pre))
    act = (pre * sig).astype(BF16)
    slope = sig * (1.0 + pre * (1.0 - sig))
    act_t = act.astype(F32).T.astype(BF16)
    x_t = x.astype(F32).T.astype(BF16)

    cot_in.wait()
    tw_in.wait()
    last = tm == tms - 1

    @pl.when(last)
    def _():
        next_cot[...] = jnp.zeros_like(next_cot)

    @pl.when(jnp.logical_not(last))
    def _():
        cot_copy.wait_recv()

    cot = cot_ref[0].reshape(pixels, chan)
    after = next_cot[...].reshape(2 * area, chan)
    later = [cot]
    for k in (1, 2):
        kept = [cot[k * area :]] if k < frames else []
        later.append(jnp.concatenate(kept + [after[: k * area]], axis=0))
    later = jnp.concatenate(later, axis=1)
    nt = (((1,), (1,)), ((), ()))
    tw = jnp.concatenate([tw_ref[k] for k in range(3)], axis=1)
    grad_act = lax.dot_general(later, tw, nt, preferred_element_type=F32).astype(BF16)
    grad_pre = (grad_act.astype(F32) * slope).astype(BF16)
    grad_pre32 = grad_pre.astype(F32)
    fill(grad_pre32, -1)

    def put(block, value):
        row = block * chan
        c = row // chunk_rows
        acc[c, pl.ds(row - c * chunk_rows, chan), :] = value

    grad_tw = jnp.dot(act_t, later, preferred_element_type=F32)
    for k in range(3):
        put(k, grad_tw[:, k * chan : (k + 1) * chan])

    def spatial_row(i):
        grad = jnp.dot(x_t, window(2 - i), preferred_element_type=F32)
        for j in range(3):
            put(3 + 3 * i + j, grad[:, j * chan : (j + 1) * chan])

    def input_grad():
        total = cot.astype(F32)
        for i in range(3):
            sw = jnp.concatenate([sw_ref[i, j] for j in range(3)], axis=1)
            total = total + lax.dot_general(window(2 - i), sw, nt, preferred_element_type=F32)
        gin_ref[0] = total.astype(BF16).reshape(frames, height, width, chan)

    offsets = [0]
    for group, scatter, _, share, _ in plan:
        offsets.append(offsets[-1] + (group_index(group) * share if scatter else 0))
    pending = []

    def start(copy):
        copy.start()
        pending.append(copy)
        return copy

    waiting = {}

    def share_at(index, share):
        return pl.ds(pl.multiple_of(index * share, TILE), share)

    def reduce_start(c, p):
        group, scatter, rows, share, kind = plan[p]
        cur, stage, recv, bsend, brecv = phases[p][:5]
        ss, rs, bss, brs = phases[p][6:10]
        index = group_index(group)
        source = cur
        if p == 0:
            source = acc
        if kind != F32:
            stage[c] = source[c].astype(kind)
            outgoing = stage
        else:
            outgoing = source
        copies = []
        for m in range(1, 1 << len(group)):
            to, their = partner(group, m)
            src = outgoing.at[c, share_at(their, share)] if scatter else outgoing.at[c]
            copies.append(
                start(
                    pltpu.make_async_remote_copy(
                        src_ref=src,
                        dst_ref=recv.at[c, index],
                        send_sem=ss.at[c, m],
                        recv_sem=rs.at[c, m],
                        device_id=to,
                        device_id_type=MESH,
                    )
                )
            )
            if c == chunks - 1:
                copies.append(
                    start(
                        pltpu.make_async_remote_copy(
                            src_ref=bsend,
                            dst_ref=brecv.at[index],
                            send_sem=bss.at[m],
                            recv_sem=brs.at[m],
                            device_id=to,
                            device_id_type=MESH,
                        )
                    )
                )
        waiting[c] = copies

    def reduce_end(c, p):
        group, scatter, rows, share, kind = plan[p]
        cur, stage, recv, bsend, brecv = phases[p][:5]
        index = group_index(group)
        source = acc if p == 0 else cur
        own = source[c, share_at(index, share)] if scatter else source[c]
        recv[c, index] = own.astype(kind)
        if c == chunks - 1:
            brecv[index] = bsend[...]
        for copy in waiting[c]:
            copy.wait_recv()
        total = recv[c, 0].astype(F32)
        for n in range(1, 1 << len(group)):
            total = total + recv[c, n].astype(F32)
        if c == chunks - 1:
            bias = brecv[0]
            for n in range(1, 1 << len(group)):
                bias = bias + brecv[n]
            if p + 1 < len(plan):
                phases[p + 1][3][...] = bias
            else:
                bias_ref[...] = bias
        if p + 1 < len(plan):
            phases[p + 1][0][c] = total
        else:
            res[c, pl.ds(pl.multiple_of(offsets[-1], TILE), share)] = total.astype(BF16)

    def gather_start(c, p):
        group, scatter, rows, share, kind = plan[p]
        gs, gr = phases[p][10:12]
        copies = []
        mine = res.at[c, pl.ds(pl.multiple_of(offsets[p + 1], TILE), share)]
        for m in range(1, 1 << len(group)):
            to, _ = partner(group, m)
            copies.append(
                start(
                    pltpu.make_async_remote_copy(
                        src_ref=mine,
                        dst_ref=mine,
                        send_sem=gs.at[c, m],
                        recv_sem=gr.at[c, m],
                        device_id=to,
                        device_id_type=MESH,
                    )
                )
            )
        waiting[c] = copies

    def gather_end(c, p):
        for copy in waiting[c]:
            copy.wait_recv()

    steps = []
    for p in range(len(plan)):
        steps.append((reduce_start, reduce_end, p))
    for p in reversed(range(len(plan))):
        if plan[p][1]:
            steps.append((gather_start, gather_end, p))

    def advance(c, k):
        if k > 0:
            steps[k - 1][1](c, steps[k - 1][2])
        if k < len(steps):
            steps[k][0](c, steps[k][2])
        else:
            grads_ref[pl.ds(c * chunk_rows, chunk_rows)] = res[c]

    phases[0][3][...] = jnp.sum(grad_pre32.reshape(pixels // 8, 8, chan), axis=0)
    begun = 0
    for i in range(3):
        spatial_row(i)
        while begun < chunks and (begun + 1) * chunk_rows <= (6 + 3 * i) * chan:
            advance(begun, 0)
            begun += 1
    for step in range(1, len(steps) + chunks):
        for c in range(chunks):
            if 1 <= step - c <= len(steps):
                advance(c, step - c)
        if step == chunks:
            input_grad()
    for copy in pending:
        copy.wait_send()

    @pl.when(tm > 0)
    def _():
        cot_copy.wait_send()


def finish(cells, gin_ref, grads_ref, bias_ref, gin_out, sw_out, sb_out, tw_out, sw, sb, tw, sems):
    norm = 1.0 / float(cells) ** 0.5
    chan = gin_ref.shape[-1]
    copies = [pltpu.make_async_copy(gin_ref, gin_out, sems.at[0])]
    copies[0].start()
    for k in range(3):
        tw[k] = grads_ref[k * chan : (k + 1) * chan].astype(F32) * norm
    copies.append(pltpu.make_async_copy(tw, tw_out, sems.at[1]))
    copies[1].start()
    sb[...] = jnp.sum(bias_ref[...], axis=0, keepdims=True) * norm
    copies.append(pltpu.make_async_copy(sb, sb_out, sems.at[2]))
    copies[2].start()
    for i in range(3):
        for j in range(3):
            row = (3 + 3 * i + j) * chan
            sw[i, j] = grads_ref[row : row + chan].astype(F32) * norm
    copies.append(pltpu.make_async_copy(sw, sw_out, sems.at[3]))
    copies[3].start()
    for copy in copies:
        copy.wait()


def local(clips, tms, clip_in, cotangent, spatial_w, spatial_b, temporal_w):
    _, frames, height, width, chan = clip_in.shape
    assert frames == 2
    total_rows = 12 * chan
    chunk_rows = total_rows // CHUNKS
    plan = make_plan(clips, tms, chunk_rows)
    operands = (clip_in, cotangent, spatial_w, spatial_b.reshape(1, chan), temporal_w)
    scratch = [pltpu.VMEM(a.shape, a.dtype) for a in operands] + [
        pltpu.SemaphoreType.DMA((5,)),
        pltpu.VMEM((2, height, width, chan), BF16),
        pltpu.VMEM((frames, (height + 2) * width, 3 * chan), BF16),
        pltpu.VMEM((CHUNKS, chunk_rows, chan), F32),
        pltpu.VMEM((CHUNKS, chunk_rows, chan), BF16),
        pltpu.SemaphoreType.DMA,
        pltpu.SemaphoreType.DMA,
    ]
    for order, (group, scatter, rows, share, kind) in enumerate(plan):
        n = 1 << len(group)
        sems = pltpu.SemaphoreType.DMA((CHUNKS, n))
        scratch += [
            pltpu.VMEM((CHUNKS, rows, chan) if order else (1, 8, chan), F32),
            pltpu.VMEM((CHUNKS, rows, chan) if kind != F32 else (1, TILE, chan), BF16),
            pltpu.VMEM((CHUNKS, n, share, chan), kind),
            pltpu.VMEM((8, chan), F32),
            pltpu.VMEM((n, 8, chan), F32),
            pltpu.VMEM((8, chan), F32),
            sems,
            sems,
            pltpu.SemaphoreType.DMA((n,)),
            pltpu.SemaphoreType.DMA((n,)),
            sems,
            sems,
        ]
    vmem = pl.BlockSpec(memory_space=pltpu.VMEM)
    grad_in, grads, bias = pl.pallas_call(
        functools.partial(kernel, plan, chunk_rows, tms),
        out_shape=(
            jax.ShapeDtypeStruct(clip_in.shape, BF16),
            jax.ShapeDtypeStruct((total_rows, chan), BF16),
            jax.ShapeDtypeStruct((8, chan), F32),
        ),
        in_specs=[pl.BlockSpec(memory_space=pltpu.HBM)] * 5,
        out_specs=(vmem, vmem, vmem),
        scratch_shapes=scratch,
        compiler_params=pltpu.CompilerParams(
            collective_id=0, has_side_effects=True, vmem_limit_bytes=48 * 1024 * 1024
        ),
        name="block_backward",
    )(*[pltpu.with_memory_space_constraint(a, pltpu.HBM) for a in operands])
    hbm = pl.BlockSpec(memory_space=pltpu.HBM)
    shapes = [(clip_in.shape, BF16), (spatial_w.shape, F32), ((1, chan), F32), (temporal_w.shape, F32)]
    cells = clips * tms * frames * height * width
    grad_in, grad_sw, grad_sb, grad_tw = pl.pallas_call(
        functools.partial(finish, cells),
        out_shape=[jax.ShapeDtypeStruct(*s) for s in shapes],
        in_specs=[vmem] * 3,
        out_specs=[hbm] * 4,
        scratch_shapes=[pltpu.VMEM(*s) for s in shapes[1:]] + [pltpu.SemaphoreType.DMA((4,))],
        compiler_params=pltpu.CompilerParams(vmem_limit_bytes=24 * 1024 * 1024),
        name="finish",
    )(grad_in, grads, bias)
    return grad_in, grad_sw, grad_sb.reshape(chan), grad_tw


def solution(mesh):
    block = P("clip", "tm", None, None, None)
    return jax.shard_map(
        functools.partial(local, mesh.shape["clip"], mesh.shape["tm"]),
        mesh=mesh,
        in_specs=(block, block, P(), P(), P()),
        out_specs=(block, P(), P(), P()),
        check_vma=False,
    )
```

```python
import functools

import jax
import jax.numpy as jnp
from jax import lax
from jax.experimental import pallas as pl
from jax.experimental.pallas import tpu as pltpu
from jax.sharding import PartitionSpec as P

MESH = pl.DeviceIdType.MESH
F32, BF16 = jnp.float32, jnp.bfloat16
TILE = 16
CHUNKS = 1


def bits_of(size):
    count = size.bit_length() - 1
    assert 1 << count == size
    return count


def make_groups(clips, tms):
    clip_bits, tm_bits = bits_of(clips), bits_of(tms)
    near = [("tm", b) for b in range(tm_bits)] + [("clip", b) for b in range(1, clip_bits) if b < 2]
    far = [("clip", b) for b in range(2, clip_bits)]
    return [("clip", 0)][:clip_bits], near, far


def make_plan(clips, tms, rows):
    core, near, far = make_groups(clips, tms)
    plan = []
    for order, group in enumerate([core, near + far]):
        kind = F32 if order == 0 else BF16
        cut = len(group)
        while rows % (TILE << cut):
            cut -= 1
        if cut:
            plan.append((tuple(group[:cut]), True, rows, rows >> cut, kind))
            rows >>= cut
        if cut < len(group):
            plan.append((tuple(group[cut:]), False, rows, rows, kind))
    return plan


def kernel(plan, bias_groups, chunk_rows, tms, *refs):
    operands = refs[:5]
    gin_ref, grads_ref, bias_ref = refs[5:8]
    x_ref, cot_ref, sw_ref, sb_ref, tw_ref = held = refs[8:13]
    held_sems = refs[13]
    next_cot, pad3, acc, res, cot_send, cot_recv = refs[14:20]
    phases, position = [], 20
    for _ in plan:
        phases.append(refs[position : position + 7])
        position += 7
    bias_parts = []
    for _ in bias_groups:
        bias_parts.append(refs[position : position + 4])
        position += 4
    frames, height, width, chan = x_ref.shape[1:]
    area = height * width
    pixels = frames * area
    chunks = acc.shape[0]
    me = {"clip": lax.axis_index("clip"), "tm": lax.axis_index("tm")}

    bits = {}
    for axis, size in (("clip", lax.axis_size("clip")), ("tm", tms)):
        for b in range(bits_of(size)):
            bits[axis, b] = lax.rem(me[axis] // (1 << b), 2)

    def group_index(group):
        return sum((bits[w] * (1 << n) for n, w in enumerate(group)), 0)

    def partner(group, m):
        to = dict(me)
        index = group_index(group)
        for n, which in enumerate(group):
            if (m >> n) & 1:
                axis, b = which
                step = 1 - 2 * bits[which]
                to[axis] = to[axis] + step * (1 << b)
                index = index + step * (1 << n)
        return to, index

    barrier = pltpu.get_barrier_semaphore()
    greeted = set()
    for group in [group for group, *_ in plan] + list(bias_groups):
        for m in range(1, 1 << len(group)):
            key = frozenset(w for n, w in enumerate(group) if (m >> n) & 1)
            if key not in greeted:
                greeted.add(key)
                pl.semaphore_signal(
                    barrier, inc=1, device_id=partner(group, m)[0], device_id_type=MESH
                )
    x_in, cot_in, sw_in, sb_in, tw_in = fetch = [
        pltpu.make_async_copy(operand, copy, held_sems.at[n])
        for n, (operand, copy) in enumerate(zip(operands, held))
    ]
    for n in (0, 2, 3, 1, 4):
        fetch[n].start()
    pl.semaphore_wait(barrier, len(greeted))

    tm = me["tm"]
    cot_copy = pltpu.make_async_remote_copy(
        src_ref=operands[1].at[0, pl.ds(0, 2)],
        dst_ref=next_cot,
        send_sem=cot_send,
        recv_sem=cot_recv,
        device_id={"clip": me["clip"], "tm": jnp.maximum(tm - 1, 0)},
        device_id_type=MESH,
    )

    @pl.when(tm > 0)
    def _():
        cot_copy.start()

    column = lax.broadcasted_iota(jnp.int32, (pixels, chan), 0) % width

    def column_shift(flat, d):
        if d == 0:
            return flat.astype(BF16)
        rolled = pltpu.roll(flat, (-d) % pixels, 0)
        edge = width - 1 if d == 1 else 0
        return jnp.where(column == edge, 0.0, rolled).astype(BF16)

    def fill(flat, sign):
        for j in range(3):
            moved = column_shift(flat, sign * (j - 1)).reshape(frames, area, chan)
            pad3[:, pl.ds(width, area), pl.ds(j * chan, chan)] = moved

    def window(start):
        return pad3[:, pl.ds(start * width, area), :].reshape(pixels, 3 * chan)

    blank = jnp.zeros((frames, width, 3 * chan), BF16)
    pad3[:, pl.ds(0, width), :] = blank
    pad3[:, pl.ds(width + area, width), :] = blank

    x_in.wait()
    x = x_ref[0].reshape(pixels, chan)
    fill(x.astype(F32), 1)
    sw_in.wait()
    sb_in.wait()
    pre = jnp.zeros((pixels, chan), F32)
    for i in range(3):
        pre = pre + jnp.dot(
            window(i), sw_ref[i].reshape(3 * chan, chan), preferred_element_type=F32
        )
    pre = pre + sb_ref[...]
    sig = 1.0 / (1.0 + jnp.exp(-pre))
    act = (pre * sig).astype(BF16)
    slope = sig * (1.0 + pre * (1.0 - sig))
    act_t = act.astype(F32).T.astype(BF16)
    x_t = x.astype(F32).T.astype(BF16)

    cot_in.wait()
    tw_in.wait()
    last = tm == tms - 1

    @pl.when(last)
    def _():
        next_cot[...] = jnp.zeros_like(next_cot)

    @pl.when(jnp.logical_not(last))
    def _():
        cot_copy.wait_recv()

    cot = cot_ref[0].reshape(pixels, chan)
    after = next_cot[...].reshape(2 * area, chan)
    later = [cot]
    for k in (1, 2):
        kept = [cot[k * area :]] if k < frames else []
        later.append(jnp.concatenate(kept + [after[: k * area]], axis=0))
    later = jnp.concatenate(later, axis=1)
    nt = (((1,), (1,)), ((), ()))
    tw = jnp.concatenate([tw_ref[k] for k in range(3)], axis=1)
    grad_act = lax.dot_general(later, tw, nt, preferred_element_type=F32).astype(BF16)
    grad_pre = (grad_act.astype(F32) * slope).astype(BF16)
    grad_pre32 = grad_pre.astype(F32)
    fill(grad_pre32, -1)

    def put(block, value):
        row = block * chan
        c = row // chunk_rows
        acc[c, pl.ds(row - c * chunk_rows, chan), :] = value

    grad_tw = jnp.dot(act_t, later, preferred_element_type=F32)
    for k in range(3):
        put(k, grad_tw[:, k * chan : (k + 1) * chan])

    def spatial_row(i):
        grad = jnp.dot(x_t, window(2 - i), preferred_element_type=F32)
        for j in range(3):
            put(3 + 3 * i + j, grad[:, j * chan : (j + 1) * chan])

    def input_grad():
        total = cot.astype(F32)
        for i in range(3):
            sw = jnp.concatenate([sw_ref[i, j] for j in range(3)], axis=1)
            total = total + lax.dot_general(window(2 - i), sw, nt, preferred_element_type=F32)
        gin_ref[0] = total.astype(BF16).reshape(frames, height, width, chan)

    offsets = [0]
    for group, scatter, _, share, _ in plan:
        offsets.append(offsets[-1] + (group_index(group) * share if scatter else 0))
    pending = []

    def start(copy):
        copy.start()
        pending.append(copy)
        return copy

    waiting = {}

    def share_at(index, share):
        return pl.ds(pl.multiple_of(index * share, TILE), share)

    def reduce_start(c, p):
        group, scatter, rows, share, kind = plan[p]
        cur, stage, recv, ss, rs = phases[p][:5]
        index = group_index(group)
        source = cur
        if p == 0:
            source = acc
        if kind != F32:
            stage[c] = source[c].astype(kind)
            outgoing = stage
        else:
            outgoing = source
        copies = []
        for m in reversed(range(1, 1 << len(group))):
            to, their = partner(group, m)
            src = outgoing.at[c, share_at(their, share)] if scatter else outgoing.at[c]
            copies.append(
                start(
                    pltpu.make_async_remote_copy(
                        src_ref=src,
                        dst_ref=recv.at[c, index],
                        send_sem=ss.at[c, m],
                        recv_sem=rs.at[c, m],
                        device_id=to,
                        device_id_type=MESH,
                    )
                )
            )
        waiting[c] = copies

    def reduce_end(c, p):
        group, scatter, rows, share, kind = plan[p]
        cur, stage, recv = phases[p][:3]
        index = group_index(group)
        source = acc if p == 0 else cur
        own = source[c, share_at(index, share)] if scatter else source[c]
        recv[c, index] = own.astype(kind)
        for copy in waiting[c]:
            copy.wait_recv()
        total = recv[c, 0].astype(F32)
        for n in range(1, 1 << len(group)):
            total = total + recv[c, n].astype(F32)
        if p + 1 < len(plan):
            phases[p + 1][0][c] = total
        else:
            res[c, pl.ds(pl.multiple_of(offsets[-1], TILE), share)] = total.astype(BF16)

    def gather_start(c, p):
        group, scatter, rows, share, kind = plan[p]
        gs, gr = phases[p][5:7]
        copies = []
        mine = res.at[c, pl.ds(pl.multiple_of(offsets[p + 1], TILE), share)]
        for m in reversed(range(1, 1 << len(group))):
            to, _ = partner(group, m)
            copies.append(
                start(
                    pltpu.make_async_remote_copy(
                        src_ref=mine,
                        dst_ref=mine,
                        send_sem=gs.at[c, m],
                        recv_sem=gr.at[c, m],
                        device_id=to,
                        device_id_type=MESH,
                    )
                )
            )
        waiting[c] = copies

    def gather_end(c, p):
        for copy in waiting[c]:
            copy.wait_recv()

    bias_waiting = []

    def bias_start(q):
        send, recv, bss, brs = bias_parts[q]
        group = bias_groups[q]
        index = group_index(group)
        for m in range(1, 1 << len(group)):
            bias_waiting.append(
                start(
                    pltpu.make_async_remote_copy(
                        src_ref=send,
                        dst_ref=recv.at[index],
                        send_sem=bss.at[m],
                        recv_sem=brs.at[m],
                        device_id=partner(group, m)[0],
                        device_id_type=MESH,
                    )
                )
            )

    def bias_end(q):
        send, recv = bias_parts[q][:2]
        recv[group_index(bias_groups[q])] = send[...]
        while bias_waiting:
            bias_waiting.pop().wait_recv()
        total = recv[0]
        for n in range(1, 1 << len(bias_groups[q])):
            total = total + recv[n]
        if q + 1 < len(bias_groups):
            bias_parts[q + 1][0][...] = total
            bias_start(q + 1)
        else:
            bias_ref[...] = total

    bias_left = list(range(len(bias_groups)))

    steps = []
    for p in range(len(plan)):
        steps.append((reduce_start, reduce_end, p))
    for p in reversed(range(len(plan))):
        if plan[p][1]:
            steps.append((gather_start, gather_end, p))

    def advance(c, k):
        if k > 0:
            steps[k - 1][1](c, steps[k - 1][2])
        if k < len(steps):
            steps[k][0](c, steps[k][2])
        else:
            grads_ref[pl.ds(c * chunk_rows, chunk_rows)] = res[c]

    bias_parts[0][0][...] = jnp.sum(grad_pre32.reshape(pixels // 8, 8, chan), axis=0)
    begun = 0
    for i in range(3):
        spatial_row(i)
        while begun < chunks and (begun + 1) * chunk_rows <= (6 + 3 * i) * chan:
            advance(begun, 0)
            begun += 1
    bias_start(0)
    for step in range(1, len(steps) + chunks):
        for c in range(chunks):
            if 1 <= step - c <= len(steps):
                advance(c, step - c)
        if step == chunks:
            input_grad()
        for q in bias_left[:2]:
            bias_end(bias_left.pop(0))
    for q in bias_left:
        bias_end(q)
    for copy in pending:
        copy.wait_send()

    @pl.when(tm > 0)
    def _():
        cot_copy.wait_send()


def finish(cells, gin_ref, grads_ref, bias_ref, gin_out, sw_out, sb_out, tw_out, sw, sb, tw, sems):
    norm = 1.0 / float(cells) ** 0.5
    chan = gin_ref.shape[-1]
    copies = [pltpu.make_async_copy(gin_ref, gin_out, sems.at[0])]
    copies[0].start()
    for k in range(3):
        tw[k] = grads_ref[k * chan : (k + 1) * chan].astype(F32) * norm
    copies.append(pltpu.make_async_copy(tw, tw_out, sems.at[1]))
    copies[1].start()
    sb[...] = jnp.sum(bias_ref[...], axis=0, keepdims=True) * norm
    copies.append(pltpu.make_async_copy(sb, sb_out, sems.at[2]))
    copies[2].start()
    for i in range(3):
        for j in range(3):
            row = (3 + 3 * i + j) * chan
            sw[i, j] = grads_ref[row : row + chan].astype(F32) * norm
    copies.append(pltpu.make_async_copy(sw, sw_out, sems.at[3]))
    copies[3].start()
    for copy in copies:
        copy.wait()


def local(clips, tms, clip_in, cotangent, spatial_w, spatial_b, temporal_w):
    _, frames, height, width, chan = clip_in.shape
    assert frames == 2
    total_rows = 12 * chan
    chunk_rows = total_rows // CHUNKS
    plan = make_plan(clips, tms, chunk_rows)
    bias_groups = [tuple(g) for g in make_groups(clips, tms) if g]
    operands = (clip_in, cotangent, spatial_w, spatial_b.reshape(1, chan), temporal_w)
    scratch = [pltpu.VMEM(a.shape, a.dtype) for a in operands] + [
        pltpu.SemaphoreType.DMA((5,)),
        pltpu.VMEM((2, height, width, chan), BF16),
        pltpu.VMEM((frames, (height + 2) * width, 3 * chan), BF16),
        pltpu.VMEM((CHUNKS, chunk_rows, chan), F32),
        pltpu.VMEM((CHUNKS, chunk_rows, chan), BF16),
        pltpu.SemaphoreType.DMA,
        pltpu.SemaphoreType.DMA,
    ]
    for order, (group, scatter, rows, share, kind) in enumerate(plan):
        n = 1 << len(group)
        sems = pltpu.SemaphoreType.DMA((CHUNKS, n))
        scratch += [
            pltpu.VMEM((CHUNKS, rows, chan) if order else (1, 8, chan), F32),
            pltpu.VMEM((CHUNKS, rows, chan) if kind != F32 else (1, TILE, chan), BF16),
            pltpu.VMEM((CHUNKS, n, share, chan), kind),
            sems,
            sems,
            sems,
            sems,
        ]
    for group in bias_groups:
        n = 1 << len(group)
        scratch += [
            pltpu.VMEM((8, chan), F32),
            pltpu.VMEM((n, 8, chan), F32),
            pltpu.SemaphoreType.DMA((n,)),
            pltpu.SemaphoreType.DMA((n,)),
        ]
    vmem = pl.BlockSpec(memory_space=pltpu.VMEM)
    grad_in, grads, bias = pl.pallas_call(
        functools.partial(kernel, plan, bias_groups, chunk_rows, tms),
        out_shape=(
            jax.ShapeDtypeStruct(clip_in.shape, BF16),
            jax.ShapeDtypeStruct((total_rows, chan), BF16),
            jax.ShapeDtypeStruct((8, chan), F32),
        ),
        in_specs=[pl.BlockSpec(memory_space=pltpu.HBM)] * 5,
        out_specs=(vmem, vmem, vmem),
        scratch_shapes=scratch,
        compiler_params=pltpu.CompilerParams(
            collective_id=0, has_side_effects=True, vmem_limit_bytes=48 * 1024 * 1024
        ),
        name="block_backward",
    )(*[pltpu.with_memory_space_constraint(a, pltpu.HBM) for a in operands])
    hbm = pl.BlockSpec(memory_space=pltpu.HBM)
    shapes = [(clip_in.shape, BF16), (spatial_w.shape, F32), ((1, chan), F32), (temporal_w.shape, F32)]
    cells = clips * tms * frames * height * width
    grad_in, grad_sw, grad_sb, grad_tw = pl.pallas_call(
        functools.partial(finish, cells),
        out_shape=[jax.ShapeDtypeStruct(*s) for s in shapes],
        in_specs=[vmem] * 3,
        out_specs=[hbm] * 4,
        scratch_shapes=[pltpu.VMEM(*s) for s in shapes[1:]] + [pltpu.SemaphoreType.DMA((4,))],
        compiler_params=pltpu.CompilerParams(vmem_limit_bytes=24 * 1024 * 1024),
        name="finish",
    )(grad_in, grads, bias)
    return grad_in, grad_sw, grad_sb.reshape(chan), grad_tw


def solution(mesh):
    block = P("clip", "tm", None, None, None)
    return jax.shard_map(
        functools.partial(local, mesh.shape["clip"], mesh.shape["tm"]),
        mesh=mesh,
        in_specs=(block, block, P(), P(), P()),
        out_specs=(block, P(), P(), P()),
        check_vma=False,
    )
```

```python
import functools

import jax
import jax.numpy as jnp
from jax import lax
from jax.experimental import pallas as pl
from jax.experimental.pallas import tpu as pltpu
from jax.sharding import PartitionSpec as P

MESH = pl.DeviceIdType.MESH
F32, BF16 = jnp.float32, jnp.bfloat16
TILE = 16
CHUNKS = 1


def bits_of(size):
    count = size.bit_length() - 1
    assert 1 << count == size
    return count


def make_groups(clips, tms):
    clip_bits, tm_bits = bits_of(clips), bits_of(tms)
    near = [("tm", b) for b in range(tm_bits)] + [("clip", b) for b in range(1, clip_bits) if b < 2]
    far = [("clip", b) for b in range(2, clip_bits)]
    return [("clip", 0)][:clip_bits], near, far


def make_plan(clips, tms, rows):
    core, near, far = make_groups(clips, tms)
    plan = []
    for group in [core, near + far]:
        kind = BF16
        cut = len(group)
        while rows % (TILE << cut):
            cut -= 1
        if cut:
            plan.append((tuple(group[:cut]), True, rows, rows >> cut, kind))
            rows >>= cut
        if cut < len(group):
            plan.append((tuple(group[cut:]), False, rows, rows, kind))
    return plan


def kernel(plan, bias_groups, chunk_rows, tms, *refs):
    operands = refs[:5]
    gin_ref, grads_ref, bias_ref = refs[5:8]
    x_ref, cot_ref, sw_ref, sb_ref, tw_ref = held = refs[8:13]
    held_sems = refs[13]
    next_cot, pad3, acc, res, cot_send, cot_recv = refs[14:20]
    phases, position = [], 20
    for _ in plan:
        phases.append(refs[position : position + 7])
        position += 7
    bias_parts = []
    for _ in bias_groups:
        bias_parts.append(refs[position : position + 4])
        position += 4
    frames, height, width, chan = x_ref.shape[1:]
    area = height * width
    chunks = acc.shape[0]
    me = {"clip": lax.axis_index("clip"), "tm": lax.axis_index("tm")}

    bits = {}
    for axis, size in (("clip", lax.axis_size("clip")), ("tm", tms)):
        for b in range(bits_of(size)):
            bits[axis, b] = lax.rem(me[axis] // (1 << b), 2)

    def group_index(group):
        return sum((bits[w] * (1 << n) for n, w in enumerate(group)), 0)

    def partner(group, m):
        to = dict(me)
        index = group_index(group)
        for n, which in enumerate(group):
            if (m >> n) & 1:
                axis, b = which
                step = 1 - 2 * bits[which]
                to[axis] = to[axis] + step * (1 << b)
                index = index + step * (1 << n)
        return to, index

    barrier = pltpu.get_barrier_semaphore()
    greeted = set()
    for group in [group for group, *_ in plan] + list(bias_groups):
        for m in range(1, 1 << len(group)):
            key = frozenset(w for n, w in enumerate(group) if (m >> n) & 1)
            if key not in greeted:
                greeted.add(key)
                pl.semaphore_signal(
                    barrier, inc=1, device_id=partner(group, m)[0], device_id_type=MESH
                )
    x_in, cot_in, sw_in, sb_in, tw_in = fetch = [
        pltpu.make_async_copy(operand, copy, held_sems.at[n])
        for n, (operand, copy) in enumerate(zip(operands, held))
    ]
    for n in (0, 2, 3, 1, 4):
        fetch[n].start()
    pl.semaphore_wait(barrier, len(greeted))

    tm = me["tm"]
    cot_copies = [
        pltpu.make_async_remote_copy(
            src_ref=operands[1].at[0, u],
            dst_ref=next_cot.at[u],
            send_sem=cot_send.at[u],
            recv_sem=cot_recv.at[u],
            device_id={"clip": me["clip"], "tm": jnp.maximum(tm - 1, 0)},
            device_id_type=MESH,
        )
        for u in range(frames)
    ]
    last = tm == tms - 1

    @pl.when(tm > 0)
    def _():
        for copy in cot_copies:
            copy.start()

    @pl.when(last)
    def _():
        next_cot[...] = jnp.zeros_like(next_cot)

    column = lax.broadcasted_iota(jnp.int32, (area, chan), 0) % width

    def column_shift(flat, d):
        if d == 0:
            return flat.astype(BF16)
        rolled = pltpu.roll(flat, (-d) % area, 0)
        edge = width - 1 if d == 1 else 0
        return jnp.where(column == edge, 0.0, rolled).astype(BF16)

    def fill(u, flat, sign):
        for j in range(3):
            moved = column_shift(flat, sign * (j - 1))
            pad3[u, pl.ds(width, area), pl.ds(j * chan, chan)] = moved

    def window(u, start):
        return pad3[u, pl.ds(start * width, area), :]

    x_in.wait()
    blank = jnp.zeros((frames, width, 3 * chan), BF16)
    pad3[:, pl.ds(0, width), :] = blank
    pad3[:, pl.ds(width + area, width), :] = blank

    frame_data = []
    for u in range(frames):
        x = x_ref[0, u].reshape(area, chan).astype(F32)
        fill(u, x, 1)
        if u == 0:
            sw_in.wait()
            sb_in.wait()
        pre = jnp.zeros((area, chan), F32)
        for i in range(3):
            pre = pre + jnp.dot(
                window(u, i), sw_ref[i].reshape(3 * chan, chan), preferred_element_type=F32
            )
        pre = pre + sb_ref[...]
        sig = 1.0 / (1.0 + jnp.exp(-pre))
        act = (pre * sig).astype(BF16)
        slope = sig * (1.0 + pre * (1.0 - sig))
        frame_data.append((x.T.astype(BF16), act.astype(F32).T.astype(BF16), slope))

    cot_in.wait()
    tw_in.wait()
    nt = (((1,), (1,)), ((), ()))
    tw = jnp.concatenate([tw_ref[k] for k in range(3)], axis=1)

    def cot_frame(v):
        source = cot_ref[0, v] if v < frames else next_cot[v - frames]
        return source.reshape(area, chan)

    def put(u, block, value):
        row = block * chan
        c = row // chunk_rows
        at = (c, pl.ds(row - c * chunk_rows, chan), slice(None))
        acc[at] = value if u == 0 else acc[at] + value

    def frame_back(u):
        x_t, act_t, slope = frame_data[u]

        @pl.when(jnp.logical_not(last))
        def _():
            cot_copies[u].wait_recv()

        later = jnp.concatenate([cot_frame(u + k) for k in range(3)], axis=1)
        grad_act = lax.dot_general(later, tw, nt, preferred_element_type=F32).astype(BF16)
        grad_pre = (grad_act.astype(F32) * slope).astype(BF16).astype(F32)
        fill(u, grad_pre, -1)
        grad_tw = jnp.dot(act_t, later, preferred_element_type=F32)
        for k in range(3):
            put(u, k, grad_tw[:, k * chan : (k + 1) * chan])
        for i in range(3):
            grad = jnp.dot(x_t, window(u, 2 - i), preferred_element_type=F32)
            for j in range(3):
                put(u, 3 + 3 * i + j, grad[:, j * chan : (j + 1) * chan])
        bias = jnp.sum(grad_pre.reshape(area // 8, 8, chan), axis=0)
        part = bias_parts[0][0]
        part[...] = bias if u == 0 else part[...] + bias

    def input_grad(u):
        total = cot_frame(u).astype(F32)
        for i in range(3):
            sw = jnp.concatenate([sw_ref[i, j] for j in range(3)], axis=1)
            total = total + lax.dot_general(window(u, 2 - i), sw, nt, preferred_element_type=F32)
        gin_ref[0, u] = total.astype(BF16).reshape(height, width, chan)

    offsets = [0]
    for group, scatter, _, share, _ in plan:
        offsets.append(offsets[-1] + (group_index(group) * share if scatter else 0))
    pending = []

    def start(copy):
        copy.start()
        pending.append(copy)
        return copy

    waiting = {}

    def share_at(index, share):
        return pl.ds(pl.multiple_of(index * share, TILE), share)

    def reduce_start(c, p):
        group, scatter, rows, share, kind = plan[p]
        cur, stage, recv, ss, rs = phases[p][:5]
        index = group_index(group)
        source = cur
        if p == 0:
            source = acc
        if kind != F32:
            if scatter and len(group) == 1:
                theirs = share_at(partner(group, 1)[1], share)
                stage[c, theirs] = source[c, theirs].astype(kind)
            else:
                stage[c] = source[c].astype(kind)
            outgoing = stage
        else:
            outgoing = source
        copies = []
        for m in reversed(range(1, 1 << len(group))):
            to, their = partner(group, m)
            src = outgoing.at[c, share_at(their, share)] if scatter else outgoing.at[c]
            copies.append(
                start(
                    pltpu.make_async_remote_copy(
                        src_ref=src,
                        dst_ref=recv.at[c, index],
                        send_sem=ss.at[c, m],
                        recv_sem=rs.at[c, m],
                        device_id=to,
                        device_id_type=MESH,
                    )
                )
            )
        waiting[c] = copies

    def reduce_end(c, p):
        group, scatter, rows, share, kind = plan[p]
        cur, stage, recv = phases[p][:3]
        index = group_index(group)
        source = acc if p == 0 else cur
        own = source[c, share_at(index, share)] if scatter else source[c]
        for copy in waiting[c]:
            copy.wait_recv()
        recv[c, index] = own.astype(kind)
        total = recv[c, 0].astype(F32)
        for n in range(1, 1 << len(group)):
            total = total + recv[c, n].astype(F32)
        if p + 1 < len(plan):
            phases[p + 1][0][c] = total
        else:
            res[c, pl.ds(pl.multiple_of(offsets[-1], TILE), share)] = total.astype(BF16)

    def gather_start(c, p):
        group, scatter, rows, share, kind = plan[p]
        gs, gr = phases[p][5:7]
        copies = []
        mine = res.at[c, pl.ds(pl.multiple_of(offsets[p + 1], TILE), share)]
        for m in reversed(range(1, 1 << len(group))):
            to, _ = partner(group, m)
            copies.append(
                start(
                    pltpu.make_async_remote_copy(
                        src_ref=mine,
                        dst_ref=mine,
                        send_sem=gs.at[c, m],
                        recv_sem=gr.at[c, m],
                        device_id=to,
                        device_id_type=MESH,
                    )
                )
            )
        waiting[c] = copies

    def gather_end(c, p):
        for copy in waiting[c]:
            copy.wait_recv()

    bias_waiting = []

    def bias_start(q):
        send, recv, bss, brs = bias_parts[q]
        group = bias_groups[q]
        index = group_index(group)
        for m in range(1, 1 << len(group)):
            bias_waiting.append(
                start(
                    pltpu.make_async_remote_copy(
                        src_ref=send,
                        dst_ref=recv.at[index],
                        send_sem=bss.at[m],
                        recv_sem=brs.at[m],
                        device_id=partner(group, m)[0],
                        device_id_type=MESH,
                    )
                )
            )

    def bias_end(q):
        send, recv = bias_parts[q][:2]
        recv[group_index(bias_groups[q])] = send[...]
        while bias_waiting:
            bias_waiting.pop().wait_recv()
        total = recv[0]
        for n in range(1, 1 << len(bias_groups[q])):
            total = total + recv[n]
        if q + 1 < len(bias_groups):
            bias_parts[q + 1][0][...] = total
            bias_start(q + 1)
        else:
            bias_ref[...] = total

    bias_left = list(range(len(bias_groups)))

    steps = []
    for p in range(len(plan)):
        steps.append((reduce_start, reduce_end, p))
    for p in reversed(range(len(plan))):
        if plan[p][1]:
            steps.append((gather_start, gather_end, p))

    def advance(c, k):
        if k > 0:
            steps[k - 1][1](c, steps[k - 1][2])
        if k < len(steps):
            steps[k][0](c, steps[k][2])
        else:
            grads_ref[pl.ds(c * chunk_rows, chunk_rows)] = res[c]

    for u in range(frames):
        frame_back(u)
        if u + 1 < frames:
            input_grad(u)
    for c in range(chunks):
        advance(c, 0)
    bias_start(0)
    for step in range(1, len(steps) + chunks):
        for c in range(chunks):
            if 1 <= step - c <= len(steps):
                advance(c, step - c)
        if step == chunks:
            input_grad(frames - 1)
        for q in bias_left[:2]:
            bias_end(bias_left.pop(0))
    for q in bias_left:
        bias_end(q)
    for copy in pending:
        copy.wait_send()

    @pl.when(tm > 0)
    def _():
        for copy in cot_copies:
            copy.wait_send()


def finish(cells, gin_ref, grads_ref, bias_ref, gin_out, sw_out, sb_out, tw_out, sw, sb, tw, sems):
    norm = 1.0 / float(cells) ** 0.5
    chan = gin_ref.shape[-1]
    copies = [pltpu.make_async_copy(gin_ref, gin_out, sems.at[0])]
    copies[0].start()
    for k in range(3):
        tw[k] = grads_ref[k * chan : (k + 1) * chan].astype(F32) * norm
    copies.append(pltpu.make_async_copy(tw, tw_out, sems.at[1]))
    copies[1].start()
    sb[...] = jnp.sum(bias_ref[...], axis=0, keepdims=True) * norm
    copies.append(pltpu.make_async_copy(sb, sb_out, sems.at[2]))
    copies[2].start()
    for i in range(3):
        for j in range(3):
            row = (3 + 3 * i + j) * chan
            sw[i, j] = grads_ref[row : row + chan].astype(F32) * norm
    copies.append(pltpu.make_async_copy(sw, sw_out, sems.at[3]))
    copies[3].start()
    for copy in copies:
        copy.wait()


def local(clips, tms, clip_in, cotangent, spatial_w, spatial_b, temporal_w):
    _, frames, height, width, chan = clip_in.shape
    assert frames == 2
    total_rows = 12 * chan
    chunk_rows = total_rows // CHUNKS
    plan = make_plan(clips, tms, chunk_rows)
    bias_groups = [tuple(g) for g in make_groups(clips, tms) if g]
    operands = (clip_in, cotangent, spatial_w, spatial_b.reshape(1, chan), temporal_w)
    scratch = [pltpu.VMEM(a.shape, a.dtype) for a in operands] + [
        pltpu.SemaphoreType.DMA((5,)),
        pltpu.VMEM((2, height, width, chan), BF16),
        pltpu.VMEM((frames, (height + 2) * width, 3 * chan), BF16),
        pltpu.VMEM((CHUNKS, chunk_rows, chan), F32),
        pltpu.VMEM((CHUNKS, chunk_rows, chan), BF16),
        pltpu.SemaphoreType.DMA((2,)),
        pltpu.SemaphoreType.DMA((2,)),
    ]
    for order, (group, scatter, rows, share, kind) in enumerate(plan):
        n = 1 << len(group)
        sems = pltpu.SemaphoreType.DMA((CHUNKS, n))
        scratch += [
            pltpu.VMEM((CHUNKS, rows, chan) if order else (1, 8, chan), F32),
            pltpu.VMEM((CHUNKS, rows, chan) if kind != F32 else (1, TILE, chan), BF16),
            pltpu.VMEM((CHUNKS, n, share, chan), kind),
            sems,
            sems,
            sems,
            sems,
        ]
    for group in bias_groups:
        n = 1 << len(group)
        scratch += [
            pltpu.VMEM((8, chan), F32),
            pltpu.VMEM((n, 8, chan), F32),
            pltpu.SemaphoreType.DMA((n,)),
            pltpu.SemaphoreType.DMA((n,)),
        ]
    vmem = pl.BlockSpec(memory_space=pltpu.VMEM)
    grad_in, grads, bias = pl.pallas_call(
        functools.partial(kernel, plan, bias_groups, chunk_rows, tms),
        out_shape=(
            jax.ShapeDtypeStruct(clip_in.shape, BF16),
            jax.ShapeDtypeStruct((total_rows, chan), BF16),
            jax.ShapeDtypeStruct((8, chan), F32),
        ),
        in_specs=[pl.BlockSpec(memory_space=pltpu.HBM)] * 5,
        out_specs=(vmem, vmem, vmem),
        scratch_shapes=scratch,
        compiler_params=pltpu.CompilerParams(
            collective_id=0, has_side_effects=True, vmem_limit_bytes=48 * 1024 * 1024
        ),
        name="block_backward",
    )(*[pltpu.with_memory_space_constraint(a, pltpu.HBM) for a in operands])
    hbm = pl.BlockSpec(memory_space=pltpu.HBM)
    shapes = [(clip_in.shape, BF16), (spatial_w.shape, F32), ((1, chan), F32), (temporal_w.shape, F32)]
    cells = clips * tms * frames * height * width
    grad_in, grad_sw, grad_sb, grad_tw = pl.pallas_call(
        functools.partial(finish, cells),
        out_shape=[jax.ShapeDtypeStruct(*s) for s in shapes],
        in_specs=[vmem] * 3,
        out_specs=[hbm] * 4,
        scratch_shapes=[pltpu.VMEM(*s) for s in shapes[1:]] + [pltpu.SemaphoreType.DMA((4,))],
        compiler_params=pltpu.CompilerParams(vmem_limit_bytes=24 * 1024 * 1024),
        name="finish",
    )(grad_in, grads, bias)
    return grad_in, grad_sw, grad_sb.reshape(chan), grad_tw


def solution(mesh):
    block = P("clip", "tm", None, None, None)
    return jax.shard_map(
        functools.partial(local, mesh.shape["clip"], mesh.shape["tm"]),
        mesh=mesh,
        in_specs=(block, block, P(), P(), P()),
        out_specs=(block, P(), P(), P()),
        check_vma=False,
    )
```

```python
import functools

import jax
import jax.numpy as jnp
from jax import lax
from jax.experimental import pallas as pl
from jax.experimental.pallas import tpu as pltpu
from jax.sharding import PartitionSpec as P

MESH = pl.DeviceIdType.MESH
F32, BF16 = jnp.float32, jnp.bfloat16
TILE = 16
CHUNKS = 1


def bits_of(size):
    count = size.bit_length() - 1
    assert 1 << count == size
    return count


def make_groups(clips, tms):
    clip_bits, tm_bits = bits_of(clips), bits_of(tms)
    near = [("tm", b) for b in range(tm_bits)] + [("clip", b) for b in range(1, clip_bits) if b < 2]
    far = [("clip", b) for b in range(2, clip_bits)]
    return [("clip", 0)][:clip_bits], near, far


def make_plan(clips, tms, rows):
    core, near, far = make_groups(clips, tms)
    plan = []
    for group in [core, near + far]:
        kind = BF16
        cut = len(group)
        while rows % (TILE << cut):
            cut -= 1
        if cut:
            plan.append((tuple(group[:cut]), True, rows, rows >> cut, kind))
            rows >>= cut
        if cut < len(group):
            plan.append((tuple(group[cut:]), False, rows, rows, kind))
    return plan


def kernel(plan, bias_groups, chunk_rows, tms, *refs):
    operands = refs[:5]
    gin_ref, grads_ref, bias_ref = refs[5:8]
    x_ref, cot_ref, sw_ref, sb_ref, tw_ref = held = refs[8:13]
    held_sems = refs[13]
    next_cot, pad3, acc, res, cot_send, cot_recv = refs[14:20]
    phases, position = [], 20
    for _ in plan:
        phases.append(refs[position : position + 7])
        position += 7
    bias_parts = []
    for _ in bias_groups:
        bias_parts.append(refs[position : position + 4])
        position += 4
    frames, height, width, chan = x_ref.shape[1:]
    area = height * width
    chunks = acc.shape[0]
    me = {"clip": lax.axis_index("clip"), "tm": lax.axis_index("tm")}

    bits = {}
    for axis, size in (("clip", lax.axis_size("clip")), ("tm", tms)):
        for b in range(bits_of(size)):
            bits[axis, b] = lax.rem(me[axis] // (1 << b), 2)

    def group_index(group):
        return sum((bits[w] * (1 << n) for n, w in enumerate(group)), 0)

    def partner(group, m):
        to = dict(me)
        index = group_index(group)
        for n, which in enumerate(group):
            if (m >> n) & 1:
                axis, b = which
                step = 1 - 2 * bits[which]
                to[axis] = to[axis] + step * (1 << b)
                index = index + step * (1 << n)
        return to, index

    barrier = pltpu.get_barrier_semaphore()
    greeted = set()
    for group in [group for group, *_ in plan] + list(bias_groups):
        for m in range(1, 1 << len(group)):
            key = frozenset(w for n, w in enumerate(group) if (m >> n) & 1)
            if key not in greeted:
                greeted.add(key)
                pl.semaphore_signal(
                    barrier, inc=1, device_id=partner(group, m)[0], device_id_type=MESH
                )
    x_in, cot_in, sw_in, sb_in, tw_in = fetch = [
        pltpu.make_async_copy(operand, copy, held_sems.at[n])
        for n, (operand, copy) in enumerate(zip(operands, held))
    ]
    for n in (0, 2, 3, 1, 4):
        fetch[n].start()
    pl.semaphore_wait(barrier, len(greeted))

    tm = me["tm"]
    cot_copies = [
        pltpu.make_async_remote_copy(
            src_ref=operands[1].at[0, u],
            dst_ref=next_cot.at[u],
            send_sem=cot_send.at[u],
            recv_sem=cot_recv.at[u],
            device_id={"clip": me["clip"], "tm": jnp.maximum(tm - 1, 0)},
            device_id_type=MESH,
        )
        for u in range(frames)
    ]
    last = tm == tms - 1

    @pl.when(tm > 0)
    def _():
        for copy in cot_copies:
            copy.start()

    @pl.when(last)
    def _():
        next_cot[...] = jnp.zeros_like(next_cot)

    column = lax.broadcasted_iota(jnp.int32, (area, chan), 0) % width

    def column_shift(flat, d):
        if d == 0:
            return flat.astype(BF16)
        rolled = pltpu.roll(flat, (-d) % area, 0)
        edge = width - 1 if d == 1 else 0
        return jnp.where(column == edge, 0.0, rolled).astype(BF16)

    def fill(u, flat, sign):
        for j in range(3):
            moved = column_shift(flat, sign * (j - 1))
            pad3[u, pl.ds(width, area), pl.ds(j * chan, chan)] = moved

    def window(u, start):
        return pad3[u, pl.ds(start * width, area), :]

    x_in.wait()
    blank = jnp.zeros((frames, width, 3 * chan), BF16)
    pad3[:, pl.ds(0, width), :] = blank
    pad3[:, pl.ds(width + area, width), :] = blank

    frame_data = []
    for u in range(frames):
        x = x_ref[0, u].reshape(area, chan).astype(F32)
        fill(u, x, 1)
        if u == 0:
            sw_in.wait()
            sb_in.wait()
        pre = jnp.zeros((area, chan), F32)
        for i in range(3):
            pre = pre + jnp.dot(
                window(u, i), sw_ref[i].reshape(3 * chan, chan), preferred_element_type=F32
            )
        pre = pre + sb_ref[...]
        sig = 1.0 / (1.0 + jnp.exp(-pre))
        act = (pre * sig).astype(BF16)
        slope = sig * (1.0 + pre * (1.0 - sig))
        frame_data.append((x.T.astype(BF16), act.astype(F32).T.astype(BF16), slope))

    cot_in.wait()
    tw_in.wait()
    nt = (((1,), (1,)), ((), ()))
    tw = jnp.concatenate([tw_ref[k] for k in range(3)], axis=1)

    def cot_frame(v):
        source = cot_ref[0, v] if v < frames else next_cot[v - frames]
        return source.reshape(area, chan)

    def put(u, block, value):
        row = block * chan
        c = row // chunk_rows
        at = (c, pl.ds(row - c * chunk_rows, chan), slice(None))
        acc[at] = value if u == 0 else acc[at] + value

    def frame_back(u):
        x_t, act_t, slope = frame_data[u]

        @pl.when(jnp.logical_not(last))
        def _():
            cot_copies[u].wait_recv()

        later = jnp.concatenate([cot_frame(u + k) for k in range(3)], axis=1)
        grad_act = lax.dot_general(later, tw, nt, preferred_element_type=F32).astype(BF16)
        grad_pre = (grad_act.astype(F32) * slope).astype(BF16).astype(F32)
        fill(u, grad_pre, -1)
        grad_tw = jnp.dot(act_t, later, preferred_element_type=F32)
        for k in range(3):
            put(u, k, grad_tw[:, k * chan : (k + 1) * chan])
        for i in range(3):
            grad = jnp.dot(x_t, window(u, 2 - i), preferred_element_type=F32)
            for j in range(3):
                put(u, 3 + 3 * i + j, grad[:, j * chan : (j + 1) * chan])
        bias = jnp.sum(grad_pre.reshape(area // 8, 8, chan), axis=0)
        part = bias_parts[0][0]
        part[...] = bias if u == 0 else part[...] + bias

    def input_grad(u):
        total = cot_frame(u).astype(F32)
        for i in range(3):
            sw = jnp.concatenate([sw_ref[i, j] for j in range(3)], axis=1)
            total = total + lax.dot_general(window(u, 2 - i), sw, nt, preferred_element_type=F32)
        gin_ref[0, u] = total.astype(BF16).reshape(height, width, chan)

    offsets = [0]
    for group, scatter, _, share, _ in plan:
        offsets.append(offsets[-1] + (group_index(group) * share if scatter else 0))
    pending = []

    def start(copy):
        copy.start()
        pending.append(copy)
        return copy

    waiting = {}

    def share_at(index, share):
        return pl.ds(pl.multiple_of(index * share, TILE), share)

    def reduce_start(c, p):
        group, scatter, rows, share, kind = plan[p]
        cur, stage, recv, ss, rs = phases[p][:5]
        index = group_index(group)
        source = cur
        if p == 0:
            source = acc
        if kind != F32:
            if scatter and len(group) == 1:
                theirs = share_at(partner(group, 1)[1], share)
                stage[c, theirs] = source[c, theirs].astype(kind)
            else:
                stage[c] = source[c].astype(kind)
            outgoing = stage
        else:
            outgoing = source
        copies = []
        if scatter and len(group) > 1:
            half = 1 << (len(group) - 1)
            low = group_index(group[:-1])
            for other in (half, 0):
                for m in range(1, half):
                    share_of = share_at(partner(group, m + other)[1], share)
                    copies.append(
                        start(
                            pltpu.make_async_remote_copy(
                                src_ref=outgoing.at[c, share_of],
                                dst_ref=recv.at[c, other + low],
                                send_sem=ss.at[c, m + other],
                                recv_sem=rs.at[c, m + other],
                                device_id=partner(group, m)[0],
                                device_id_type=MESH,
                            )
                        )
                    )
            waiting[c] = copies
            return
        for m in reversed(range(1, 1 << len(group))):
            to, their = partner(group, m)
            src = outgoing.at[c, share_at(their, share)] if scatter else outgoing.at[c]
            copies.append(
                start(
                    pltpu.make_async_remote_copy(
                        src_ref=src,
                        dst_ref=recv.at[c, index],
                        send_sem=ss.at[c, m],
                        recv_sem=rs.at[c, m],
                        device_id=to,
                        device_id_type=MESH,
                    )
                )
            )
        waiting[c] = copies

    def reduce_end(c, p):
        group, scatter, rows, share, kind = plan[p]
        cur, stage, recv = phases[p][:3]
        index = group_index(group)
        source = acc if p == 0 else cur
        own = source[c, share_at(index, share)] if scatter else source[c]
        if scatter and len(group) > 1:
            total = halves_end(c, p, own)
        else:
            total = plain_end(c, p, own)
        if p + 1 < len(plan):
            phases[p + 1][0][c] = total
        else:
            res[c, pl.ds(pl.multiple_of(offsets[-1], TILE), share)] = total.astype(BF16)

    def plain_end(c, p, own):
        group, kind, recv = plan[p][0], plan[p][4], phases[p][2]
        recv[c, group_index(group)] = own.astype(kind)
        for copy in waiting[c]:
            copy.wait_recv()
        total = recv[c, 0].astype(F32)
        for n in range(1, 1 << len(group)):
            total = total + recv[c, n].astype(F32)
        return total

    def halves_end(c, p, own):
        group, _, _, share, kind = plan[p]
        cur, _, recv, ss, rs = phases[p][:5]
        source = acc if p == 0 else cur
        count = 1 << len(group)
        half = count // 2
        low = group_index(group[:-1])
        to, across = partner(group, half)
        recv[c, half + low] = source[c, share_at(across, share)].astype(kind)
        for copy in waiting[c][: half - 1]:
            copy.wait_recv()
        total = recv[c, half].astype(F32)
        for n in range(half + 1, count):
            total = total + recv[c, n].astype(F32)
        recv[c, count] = total.astype(kind)
        cross = start(
            pltpu.make_async_remote_copy(
                src_ref=recv.at[c, count],
                dst_ref=recv.at[c, count + 1],
                send_sem=ss.at[c, half],
                recv_sem=rs.at[c, half],
                device_id=to,
                device_id_type=MESH,
            )
        )
        recv[c, low] = own.astype(kind)
        for copy in waiting[c][half - 1 :]:
            copy.wait_recv()
        total = recv[c, 0].astype(F32)
        for n in range(1, half):
            total = total + recv[c, n].astype(F32)
        cross.wait_recv()
        return total + recv[c, count + 1].astype(F32)

    def gather_start(c, p):
        group, scatter, rows, share, kind = plan[p]
        gs, gr = phases[p][5:7]
        def piece(index):
            row = pl.multiple_of(offsets[p] + index * share, TILE)
            return res.at[c, pl.ds(row, share)]

        def send(index, m, sem):
            return start(
                pltpu.make_async_remote_copy(
                    src_ref=piece(index),
                    dst_ref=piece(index),
                    send_sem=gs.at[c, sem],
                    recv_sem=gr.at[c, sem],
                    device_id=partner(group, m)[0],
                    device_id_type=MESH,
                )
            )

        half = 1 << (len(group) - 1)
        index = group_index(group)
        cross = send(index, half, half)
        copies = [send(index, m, m) for m in range(1, half)]
        cross.wait_recv()
        across = partner(group, half)[1]
        copies += [send(across, m, m + half) for m in range(1, half)]
        waiting[c] = copies

    def gather_end(c, p):
        for copy in waiting[c]:
            copy.wait_recv()

    bias_waiting = []

    def bias_start(q):
        send, recv, bss, brs = bias_parts[q]
        group = bias_groups[q]
        index = group_index(group)
        for m in range(1, 1 << len(group)):
            bias_waiting.append(
                start(
                    pltpu.make_async_remote_copy(
                        src_ref=send,
                        dst_ref=recv.at[index],
                        send_sem=bss.at[m],
                        recv_sem=brs.at[m],
                        device_id=partner(group, m)[0],
                        device_id_type=MESH,
                    )
                )
            )

    def bias_end(q):
        send, recv = bias_parts[q][:2]
        recv[group_index(bias_groups[q])] = send[...]
        while bias_waiting:
            bias_waiting.pop().wait_recv()
        total = recv[0]
        for n in range(1, 1 << len(bias_groups[q])):
            total = total + recv[n]
        if q + 1 < len(bias_groups):
            bias_parts[q + 1][0][...] = total
            bias_start(q + 1)
        else:
            bias_ref[...] = total

    bias_left = list(range(len(bias_groups)))

    steps = []
    for p in range(len(plan)):
        steps.append((reduce_start, reduce_end, p))
    for p in reversed(range(len(plan))):
        if plan[p][1]:
            steps.append((gather_start, gather_end, p))

    def advance(c, k):
        if k > 0:
            steps[k - 1][1](c, steps[k - 1][2])
        if k < len(steps):
            steps[k][0](c, steps[k][2])
        else:
            grads_ref[pl.ds(c * chunk_rows, chunk_rows)] = res[c]

    for u in range(frames):
        frame_back(u)
        if u + 1 < frames:
            input_grad(u)
    for c in range(chunks):
        advance(c, 0)
    bias_start(0)
    for step in range(1, len(steps) + chunks):
        for c in range(chunks):
            if 1 <= step - c <= len(steps):
                advance(c, step - c)
        if step == chunks:
            input_grad(frames - 1)
        for q in bias_left[:1]:
            bias_end(bias_left.pop(0))
    for q in bias_left:
        bias_end(q)
    for copy in pending:
        copy.wait_send()

    @pl.when(tm > 0)
    def _():
        for copy in cot_copies:
            copy.wait_send()


def finish(cells, gin_ref, grads_ref, bias_ref, gin_out, sw_out, sb_out, tw_out, sw, sb, tw, sems):
    norm = 1.0 / float(cells) ** 0.5
    chan = gin_ref.shape[-1]
    copies = [pltpu.make_async_copy(gin_ref, gin_out, sems.at[0])]
    copies[0].start()
    for k in range(3):
        tw[k] = grads_ref[k * chan : (k + 1) * chan].astype(F32) * norm
    copies.append(pltpu.make_async_copy(tw, tw_out, sems.at[1]))
    copies[1].start()
    sb[...] = jnp.sum(bias_ref[...], axis=0, keepdims=True) * norm
    copies.append(pltpu.make_async_copy(sb, sb_out, sems.at[2]))
    copies[2].start()
    for i in range(3):
        for j in range(3):
            row = (3 + 3 * i + j) * chan
            sw[i, j] = grads_ref[row : row + chan].astype(F32) * norm
    copies.append(pltpu.make_async_copy(sw, sw_out, sems.at[3]))
    copies[3].start()
    for copy in copies:
        copy.wait()


def local(clips, tms, clip_in, cotangent, spatial_w, spatial_b, temporal_w):
    _, frames, height, width, chan = clip_in.shape
    assert frames == 2
    total_rows = 12 * chan
    chunk_rows = total_rows // CHUNKS
    plan = make_plan(clips, tms, chunk_rows)
    bias_groups = [tuple(g) for g in make_groups(clips, tms) if g]
    operands = (clip_in, cotangent, spatial_w, spatial_b.reshape(1, chan), temporal_w)
    scratch = [pltpu.VMEM(a.shape, a.dtype) for a in operands] + [
        pltpu.SemaphoreType.DMA((5,)),
        pltpu.VMEM((2, height, width, chan), BF16),
        pltpu.VMEM((frames, (height + 2) * width, 3 * chan), BF16),
        pltpu.VMEM((CHUNKS, chunk_rows, chan), F32),
        pltpu.VMEM((CHUNKS, chunk_rows, chan), BF16),
        pltpu.SemaphoreType.DMA((2,)),
        pltpu.SemaphoreType.DMA((2,)),
    ]
    for order, (group, scatter, rows, share, kind) in enumerate(plan):
        n = 1 << len(group)
        sems = pltpu.SemaphoreType.DMA((CHUNKS, n))
        scratch += [
            pltpu.VMEM((CHUNKS, rows, chan) if order else (1, 8, chan), F32),
            pltpu.VMEM((CHUNKS, rows, chan) if kind != F32 else (1, TILE, chan), BF16),
            pltpu.VMEM((CHUNKS, n + 2, share, chan), kind),
            sems,
            sems,
            sems,
            sems,
        ]
    for group in bias_groups:
        n = 1 << len(group)
        scratch += [
            pltpu.VMEM((8, chan), F32),
            pltpu.VMEM((n, 8, chan), F32),
            pltpu.SemaphoreType.DMA((n,)),
            pltpu.SemaphoreType.DMA((n,)),
        ]
    vmem = pl.BlockSpec(memory_space=pltpu.VMEM)
    grad_in, grads, bias = pl.pallas_call(
        functools.partial(kernel, plan, bias_groups, chunk_rows, tms),
        out_shape=(
            jax.ShapeDtypeStruct(clip_in.shape, BF16),
            jax.ShapeDtypeStruct((total_rows, chan), BF16),
            jax.ShapeDtypeStruct((8, chan), F32),
        ),
        in_specs=[pl.BlockSpec(memory_space=pltpu.HBM)] * 5,
        out_specs=(vmem, vmem, vmem),
        scratch_shapes=scratch,
        compiler_params=pltpu.CompilerParams(
            collective_id=0, has_side_effects=True, vmem_limit_bytes=48 * 1024 * 1024
        ),
        name="block_backward",
    )(*[pltpu.with_memory_space_constraint(a, pltpu.HBM) for a in operands])
    hbm = pl.BlockSpec(memory_space=pltpu.HBM)
    shapes = [(clip_in.shape, BF16), (spatial_w.shape, F32), ((1, chan), F32), (temporal_w.shape, F32)]
    cells = clips * tms * frames * height * width
    grad_in, grad_sw, grad_sb, grad_tw = pl.pallas_call(
        functools.partial(finish, cells),
        out_shape=[jax.ShapeDtypeStruct(*s) for s in shapes],
        in_specs=[vmem] * 3,
        out_specs=[hbm] * 4,
        scratch_shapes=[pltpu.VMEM(*s) for s in shapes[1:]] + [pltpu.SemaphoreType.DMA((4,))],
        compiler_params=pltpu.CompilerParams(vmem_limit_bytes=24 * 1024 * 1024),
        name="finish",
    )(grad_in, grads, bias)
    return grad_in, grad_sw, grad_sb.reshape(chan), grad_tw


def solution(mesh):
    block = P("clip", "tm", None, None, None)
    return jax.shard_map(
        functools.partial(local, mesh.shape["clip"], mesh.shape["tm"]),
        mesh=mesh,
        in_specs=(block, block, P(), P(), P()),
        out_specs=(block, P(), P(), P()),
        check_vma=False,
    )
```

```python
import functools

import jax
import jax.numpy as jnp
from jax import lax
from jax.experimental import pallas as pl
from jax.experimental.pallas import tpu as pltpu
from jax.sharding import PartitionSpec as P

MESH = pl.DeviceIdType.MESH
F32, BF16 = jnp.float32, jnp.bfloat16
TILE = 16
CHUNKS = 1


def bits_of(size):
    count = size.bit_length() - 1
    assert 1 << count == size
    return count


def make_groups(clips, tms):
    clip_bits, tm_bits = bits_of(clips), bits_of(tms)
    near = [("tm", b) for b in range(tm_bits)] + [("clip", b) for b in range(1, clip_bits) if b < 2]
    far = [("clip", b) for b in range(2, clip_bits)]
    return [("clip", 0)][:clip_bits], near, far


def make_plan(clips, tms, rows):
    core, near, far = make_groups(clips, tms)
    plan = []
    for group in [core, near + far]:
        kind = BF16
        cut = len(group)
        while rows % (TILE << cut):
            cut -= 1
        if cut:
            plan.append((tuple(group[:cut]), True, rows, rows >> cut, kind))
            rows >>= cut
        if cut < len(group):
            plan.append((tuple(group[cut:]), False, rows, rows, kind))
    return plan


def kernel(plan, bias_groups, chunk_rows, tms, *refs):
    operands = refs[:5]
    gin_ref, grads_ref, bias_ref = refs[5:8]
    x_ref, cot_ref, sw_ref, sb_ref, tw_ref = held = refs[8:13]
    held_sems = refs[13]
    next_cot, pad3, acc, res, cot_send, cot_recv = refs[14:20]
    phases, position = [], 20
    for _ in plan:
        phases.append(refs[position : position + 5])
        position += 5
    bias_parts = []
    for _ in bias_groups:
        bias_parts.append(refs[position : position + 4])
        position += 4
    gather_sems = refs[position:]
    frames, height, width, chan = x_ref.shape[1:]
    area = height * width
    chunks = acc.shape[0]
    me = {"clip": lax.axis_index("clip"), "tm": lax.axis_index("tm")}

    bits = {}
    for axis, size in (("clip", lax.axis_size("clip")), ("tm", tms)):
        for b in range(bits_of(size)):
            bits[axis, b] = lax.rem(me[axis] // (1 << b), 2)

    def group_index(group):
        return sum((bits[w] * (1 << n) for n, w in enumerate(group)), 0)

    def partner(group, m):
        to = dict(me)
        index = group_index(group)
        for n, which in enumerate(group):
            if (m >> n) & 1:
                axis, b = which
                step = 1 - 2 * bits[which]
                to[axis] = to[axis] + step * (1 << b)
                index = index + step * (1 << n)
        return to, index

    barrier = pltpu.get_barrier_semaphore()
    greeted = set()
    everyone = tuple(w for group, scatter, *_ in plan if scatter for w in group)
    for group in [group for group, *_ in plan] + list(bias_groups) + [everyone]:
        for m in range(1, 1 << len(group)):
            key = frozenset(w for n, w in enumerate(group) if (m >> n) & 1)
            if key not in greeted:
                greeted.add(key)
                pl.semaphore_signal(
                    barrier, inc=1, device_id=partner(group, m)[0], device_id_type=MESH
                )
    x_in, cot_in, sw_in, sb_in, tw_in = fetch = [
        pltpu.make_async_copy(operand, copy, held_sems.at[n])
        for n, (operand, copy) in enumerate(zip(operands, held))
    ]
    for n in (0, 2, 3, 1, 4):
        fetch[n].start()
    pl.semaphore_wait(barrier, len(greeted))

    tm = me["tm"]
    cot_copies = [
        pltpu.make_async_remote_copy(
            src_ref=operands[1].at[0, u],
            dst_ref=next_cot.at[u],
            send_sem=cot_send.at[u],
            recv_sem=cot_recv.at[u],
            device_id={"clip": me["clip"], "tm": jnp.maximum(tm - 1, 0)},
            device_id_type=MESH,
        )
        for u in range(frames)
    ]
    last = tm == tms - 1

    @pl.when(tm > 0)
    def _():
        for copy in cot_copies:
            copy.start()

    @pl.when(last)
    def _():
        next_cot[...] = jnp.zeros_like(next_cot)

    column = lax.broadcasted_iota(jnp.int32, (area, chan), 0) % width

    def column_shift(flat, d):
        if d == 0:
            return flat.astype(BF16)
        rolled = pltpu.roll(flat, (-d) % area, 0)
        edge = width - 1 if d == 1 else 0
        return jnp.where(column == edge, 0.0, rolled).astype(BF16)

    def fill(u, flat, sign):
        for j in range(3):
            moved = column_shift(flat, sign * (j - 1))
            pad3[u, pl.ds(width, area), pl.ds(j * chan, chan)] = moved

    def window(u, start):
        return pad3[u, pl.ds(start * width, area), :]

    x_in.wait()
    blank = jnp.zeros((frames, width, 3 * chan), BF16)
    pad3[:, pl.ds(0, width), :] = blank
    pad3[:, pl.ds(width + area, width), :] = blank

    frame_data = []
    for u in range(frames):
        x = x_ref[0, u].reshape(area, chan).astype(F32)
        fill(u, x, 1)
        if u == 0:
            sw_in.wait()
            sb_in.wait()
        pre = jnp.zeros((area, chan), F32)
        for i in range(3):
            pre = pre + jnp.dot(
                window(u, i), sw_ref[i].reshape(3 * chan, chan), preferred_element_type=F32
            )
        pre = pre + sb_ref[...]
        sig = 1.0 / (1.0 + jnp.exp(-pre))
        act = (pre * sig).astype(BF16)
        slope = sig * (1.0 + pre * (1.0 - sig))
        frame_data.append((x.T.astype(BF16), act.astype(F32).T.astype(BF16), slope))

    cot_in.wait()
    tw_in.wait()
    nt = (((1,), (1,)), ((), ()))
    tw = jnp.concatenate([tw_ref[k] for k in range(3)], axis=1)

    def cot_frame(v):
        source = cot_ref[0, v] if v < frames else next_cot[v - frames]
        return source.reshape(area, chan)

    def put(u, block, value):
        row = block * chan
        c = row // chunk_rows
        at = (c, pl.ds(row - c * chunk_rows, chan), slice(None))
        acc[at] = value if u == 0 else acc[at] + value

    def frame_back(u):
        x_t, act_t, slope = frame_data[u]

        @pl.when(jnp.logical_not(last))
        def _():
            cot_copies[u].wait_recv()

        later = jnp.concatenate([cot_frame(u + k) for k in range(3)], axis=1)
        grad_act = lax.dot_general(later, tw, nt, preferred_element_type=F32).astype(BF16)
        grad_pre = (grad_act.astype(F32) * slope).astype(BF16).astype(F32)
        fill(u, grad_pre, -1)
        grad_tw = jnp.dot(act_t, later, preferred_element_type=F32)
        for k in range(3):
            put(u, k, grad_tw[:, k * chan : (k + 1) * chan])
        for i in range(3):
            grad = jnp.dot(x_t, window(u, 2 - i), preferred_element_type=F32)
            for j in range(3):
                put(u, 3 + 3 * i + j, grad[:, j * chan : (j + 1) * chan])
        bias = jnp.sum(grad_pre.reshape(area // 8, 8, chan), axis=0)
        part = bias_parts[0][0]
        part[...] = bias if u == 0 else part[...] + bias

    def input_grad(u):
        total = cot_frame(u).astype(F32)
        for i in range(3):
            sw = jnp.concatenate([sw_ref[i, j] for j in range(3)], axis=1)
            total = total + lax.dot_general(window(u, 2 - i), sw, nt, preferred_element_type=F32)
        gin_ref[0, u] = total.astype(BF16).reshape(height, width, chan)

    offsets = [0]
    for group, scatter, _, share, _ in plan:
        offsets.append(offsets[-1] + (group_index(group) * share if scatter else 0))
    pending = []

    def start(copy):
        copy.start()
        pending.append(copy)
        return copy

    waiting = {}

    def share_at(index, share):
        return pl.ds(pl.multiple_of(index * share, TILE), share)

    def reduce_start(c, p):
        group, scatter, rows, share, kind = plan[p]
        cur, stage, recv, ss, rs = phases[p][:5]
        index = group_index(group)
        source = cur
        if p == 0:
            source = acc
        if kind != F32:
            if scatter and len(group) == 1:
                theirs = share_at(partner(group, 1)[1], share)
                stage[c, theirs] = source[c, theirs].astype(kind)
            else:
                stage[c] = source[c].astype(kind)
            outgoing = stage
        else:
            outgoing = source
        copies = []
        for m in reversed(range(1, 1 << len(group))):
            to, their = partner(group, m)
            src = outgoing.at[c, share_at(their, share)] if scatter else outgoing.at[c]
            copies.append(
                start(
                    pltpu.make_async_remote_copy(
                        src_ref=src,
                        dst_ref=recv.at[c, index],
                        send_sem=ss.at[c, m],
                        recv_sem=rs.at[c, m],
                        device_id=to,
                        device_id_type=MESH,
                    )
                )
            )
        waiting[c] = copies

    def reduce_end(c, p):
        group, scatter, rows, share, kind = plan[p]
        cur, stage, recv = phases[p][:3]
        index = group_index(group)
        source = acc if p == 0 else cur
        own = source[c, share_at(index, share)] if scatter else source[c]
        for copy in waiting[c]:
            copy.wait_recv()
        recv[c, index] = own.astype(kind)
        total = recv[c, 0].astype(F32)
        for n in range(1, 1 << len(group)):
            total = total + recv[c, n].astype(F32)
        if p + 1 < len(plan):
            phases[p + 1][0][c] = total
        else:
            res[c, pl.ds(pl.multiple_of(offsets[-1], TILE), share)] = total.astype(BF16)

    def gather_start(c, p):
        gs, gr = gather_sems
        share = plan[-1][3]
        mine = res.at[c, pl.ds(pl.multiple_of(offsets[-1], TILE), share)]
        copies = []
        for m in reversed(range(1, 1 << len(everyone))):
            copies.append(
                start(
                    pltpu.make_async_remote_copy(
                        src_ref=mine,
                        dst_ref=mine,
                        send_sem=gs.at[c, m],
                        recv_sem=gr.at[c, m],
                        device_id=partner(everyone, m)[0],
                        device_id_type=MESH,
                    )
                )
            )
        waiting[c] = copies

    def gather_end(c, p):
        for copy in waiting[c]:
            copy.wait_recv()

    bias_waiting = []

    def bias_start(q):
        send, recv, bss, brs = bias_parts[q]
        group = bias_groups[q]
        index = group_index(group)
        for m in range(1, 1 << len(group)):
            bias_waiting.append(
                start(
                    pltpu.make_async_remote_copy(
                        src_ref=send,
                        dst_ref=recv.at[index],
                        send_sem=bss.at[m],
                        recv_sem=brs.at[m],
                        device_id=partner(group, m)[0],
                        device_id_type=MESH,
                    )
                )
            )

    def bias_end(q):
        send, recv = bias_parts[q][:2]
        recv[group_index(bias_groups[q])] = send[...]
        while bias_waiting:
            bias_waiting.pop().wait_recv()
        total = recv[0]
        for n in range(1, 1 << len(bias_groups[q])):
            total = total + recv[n]
        if q + 1 < len(bias_groups):
            bias_parts[q + 1][0][...] = total
            bias_start(q + 1)
        else:
            bias_ref[...] = total

    bias_left = list(range(len(bias_groups)))

    steps = []
    for p in range(len(plan)):
        steps.append((reduce_start, reduce_end, p))
    if everyone:
        steps.append((gather_start, gather_end, 0))

    def advance(c, k):
        if k > 0:
            steps[k - 1][1](c, steps[k - 1][2])
        if k < len(steps):
            steps[k][0](c, steps[k][2])
        else:
            grads_ref[pl.ds(c * chunk_rows, chunk_rows)] = res[c]

    for u in range(frames):
        frame_back(u)
        if u + 1 < frames:
            input_grad(u)
    for c in range(chunks):
        advance(c, 0)
    bias_start(0)
    for step in range(1, len(steps) + chunks):
        for c in range(chunks):
            if 1 <= step - c <= len(steps):
                advance(c, step - c)
        if step == chunks:
            input_grad(frames - 1)
        for q in bias_left[:2]:
            bias_end(bias_left.pop(0))
    for q in bias_left:
        bias_end(q)
    for copy in pending:
        copy.wait_send()

    @pl.when(tm > 0)
    def _():
        for copy in cot_copies:
            copy.wait_send()


def finish(cells, gin_ref, grads_ref, bias_ref, gin_out, sw_out, sb_out, tw_out, sw, sb, tw, sems):
    norm = 1.0 / float(cells) ** 0.5
    chan = gin_ref.shape[-1]
    copies = [pltpu.make_async_copy(gin_ref, gin_out, sems.at[0])]
    copies[0].start()
    for k in range(3):
        tw[k] = grads_ref[k * chan : (k + 1) * chan].astype(F32) * norm
    copies.append(pltpu.make_async_copy(tw, tw_out, sems.at[1]))
    copies[1].start()
    sb[...] = jnp.sum(bias_ref[...], axis=0, keepdims=True) * norm
    copies.append(pltpu.make_async_copy(sb, sb_out, sems.at[2]))
    copies[2].start()
    for i in range(3):
        for j in range(3):
            row = (3 + 3 * i + j) * chan
            sw[i, j] = grads_ref[row : row + chan].astype(F32) * norm
    copies.append(pltpu.make_async_copy(sw, sw_out, sems.at[3]))
    copies[3].start()
    for copy in copies:
        copy.wait()


def local(clips, tms, clip_in, cotangent, spatial_w, spatial_b, temporal_w):
    _, frames, height, width, chan = clip_in.shape
    assert frames == 2
    total_rows = 12 * chan
    chunk_rows = total_rows // CHUNKS
    plan = make_plan(clips, tms, chunk_rows)
    bias_groups = [tuple(g) for g in make_groups(clips, tms) if g]
    operands = (clip_in, cotangent, spatial_w, spatial_b.reshape(1, chan), temporal_w)
    scratch = [pltpu.VMEM(a.shape, a.dtype) for a in operands] + [
        pltpu.SemaphoreType.DMA((5,)),
        pltpu.VMEM((2, height, width, chan), BF16),
        pltpu.VMEM((frames, (height + 2) * width, 3 * chan), BF16),
        pltpu.VMEM((CHUNKS, chunk_rows, chan), F32),
        pltpu.VMEM((CHUNKS, chunk_rows, chan), BF16),
        pltpu.SemaphoreType.DMA((2,)),
        pltpu.SemaphoreType.DMA((2,)),
    ]
    for order, (group, scatter, rows, share, kind) in enumerate(plan):
        n = 1 << len(group)
        sems = pltpu.SemaphoreType.DMA((CHUNKS, n))
        scratch += [
            pltpu.VMEM((CHUNKS, rows, chan) if order else (1, 8, chan), F32),
            pltpu.VMEM((CHUNKS, rows, chan) if kind != F32 else (1, TILE, chan), BF16),
            pltpu.VMEM((CHUNKS, n, share, chan), kind),
            sems,
            sems,
        ]
    for group in bias_groups:
        n = 1 << len(group)
        scratch += [
            pltpu.VMEM((8, chan), F32),
            pltpu.VMEM((n, 8, chan), F32),
            pltpu.SemaphoreType.DMA((n,)),
            pltpu.SemaphoreType.DMA((n,)),
        ]
    reached = 1 << sum(len(group) for group, scatter, *_ in plan if scatter)
    scratch += [pltpu.SemaphoreType.DMA((CHUNKS, reached))] * 2
    vmem = pl.BlockSpec(memory_space=pltpu.VMEM)
    grad_in, grads, bias = pl.pallas_call(
        functools.partial(kernel, plan, bias_groups, chunk_rows, tms),
        out_shape=(
            jax.ShapeDtypeStruct(clip_in.shape, BF16),
            jax.ShapeDtypeStruct((total_rows, chan), BF16),
            jax.ShapeDtypeStruct((8, chan), F32),
        ),
        in_specs=[pl.BlockSpec(memory_space=pltpu.HBM)] * 5,
        out_specs=(vmem, vmem, vmem),
        scratch_shapes=scratch,
        compiler_params=pltpu.CompilerParams(
            collective_id=0, has_side_effects=True, vmem_limit_bytes=48 * 1024 * 1024
        ),
        name="block_backward",
    )(*[pltpu.with_memory_space_constraint(a, pltpu.HBM) for a in operands])
    hbm = pl.BlockSpec(memory_space=pltpu.HBM)
    shapes = [(clip_in.shape, BF16), (spatial_w.shape, F32), ((1, chan), F32), (temporal_w.shape, F32)]
    cells = clips * tms * frames * height * width
    grad_in, grad_sw, grad_sb, grad_tw = pl.pallas_call(
        functools.partial(finish, cells),
        out_shape=[jax.ShapeDtypeStruct(*s) for s in shapes],
        in_specs=[vmem] * 3,
        out_specs=[hbm] * 4,
        scratch_shapes=[pltpu.VMEM(*s) for s in shapes[1:]] + [pltpu.SemaphoreType.DMA((4,))],
        compiler_params=pltpu.CompilerParams(vmem_limit_bytes=24 * 1024 * 1024),
        name="finish",
    )(grad_in, grads, bias)
    return grad_in, grad_sw, grad_sb.reshape(chan), grad_tw


def solution(mesh):
    block = P("clip", "tm", None, None, None)
    return jax.shard_map(
        functools.partial(local, mesh.shape["clip"], mesh.shape["tm"]),
        mesh=mesh,
        in_specs=(block, block, P(), P(), P()),
        out_specs=(block, P(), P(), P()),
        check_vma=False,
    )
```
